128 devices in a mesh: dp: 8 (over z, core), seq: 16 (over x, y).
Axes of the slice: x: 4, y: 4, z: 4, core: 2. Of those that a mesh axis runs over, the one named last changes fastest.
Arguments:
- queries: bfloat16 [8, 8192, 4096], P('dp', 'seq')
- latents: bfloat16 [8, 16, 64, 1280], P('dp', 'seq')
- k_weight: bfloat16 [1280, 4096], P(None, 'seq'), may hold values from -0.15625 to 0.15625
- v_weight: bfloat16 [1280, 4096], P(None, 'seq'), may hold values from -0.15625 to 0.15625
- d_context: bfloat16 [8, 8192, 4096], P('dp', 'seq'), may hold values from -6 to 6
- image_pos: int32 [8, 16], P('dp'), may hold values from 0 to 8191, as said below
- image_slot: int32 [8, 16], P('dp'), may hold values from 0 to 15, each once within a row
Outputs:
- context: bfloat16 [8, 8192, 4096], P('dp', 'seq')
- d_queries: bfloat16 [8, 8192, 4096], P('dp', 'seq')
- d_latents: bfloat16 [8, 16, 64, 1280], P('dp', 'seq')
- d_k_weight: float32 [1280, 4096], P(None, 'seq')
- d_v_weight: float32 [1280, 4096], P(None, 'seq')
The draws below stay inside these ranges and needn't reach their ends.
Inputs may be any that keep to these rules, and one draw needn't show every extreme that they name: `image_pos`: in every document the image positions rise strictly and the first is 0. The 512 tokens of one seq device attend to at most 3 images, and in every document some device attends to exactly that many. `image_slot`: each row names every slot once.
All inputs are finite; a program needn't handle non-finite values.
Results may differ from the reference program's by a relative error of at most 0.02.
Values may be sent and summed in bfloat16 or wider, within the bound.
A program may use at most 128 MiB of HBM per device.

```python
import math
import jax
import jax.numpy as jnp
from jax import lax

HEADS = 32
HD = 128
DV = 1280
LATENTS = 64
IMG_DEV = 1
TOK_DEV = 512
NEED = 3
IMAGES = 16
LENGTH = 8192
DOCS = 8


def spread_factors(factor_key, shape, top):
    return jnp.exp(jax.random.uniform(factor_key, shape, jnp.float32, 0.0, math.log(top)))


def draw_queries(key, part):
    key = jax.random.fold_in(key, 3)
    key_base, key_rows, key_cols = jax.random.split(key, 3)
    shape = (DOCS, LENGTH, HEADS, HD)
    base = jax.random.normal(key_base, shape, jnp.float32)
    row_scale = spread_factors(key_rows, (DOCS, LENGTH, HEADS, 1), 10.0)
    col_scale = spread_factors(key_cols, (1, 1, 1, HD), 5.0)
    return (base * row_scale * col_scale).reshape(DOCS, LENGTH, HEADS * HD).astype(jnp.bfloat16)


def draw_latents(key, part):
    key = jax.random.fold_in(key, 5)
    key_base, key_rows, key_cols = jax.random.split(key, 3)
    shape = (DOCS, IMAGES, LATENTS, DV)
    base = jax.random.normal(key_base, shape, jnp.float32)
    row_scale = spread_factors(key_rows, (DOCS, IMAGES, LATENTS, 1), 10.0)
    col_scale = spread_factors(key_cols, (1, 1, 1, DV), 4.0)
    return (base * row_scale * col_scale).astype(jnp.bfloat16)


def draw_image_pos(key, part):
    key = jax.random.fold_in(key, 7)
    block_total = LENGTH // TOK_DEV
    pair_total = block_total // 2
    most_starts = 2 * IMG_DEV

    def document_positions(doc_key):
        key_share, key_offsets = jax.random.split(doc_key)
        pair_share = jax.random.randint(key_share, (pair_total,), 0, most_starts + 1)
        pair_share = pair_share.at[0].set(jnp.maximum(pair_share[0], 1))
        pair_share = pair_share.at[1].set(most_starts)
        counts = jnp.stack([pair_share, most_starts - pair_share], axis=1).reshape(block_total)

        def block_offsets(block_key, count):
            shuffled = jax.random.permutation(block_key, TOK_DEV - 1) + 1
            chosen = jnp.where(jnp.arange(most_starts) < count, shuffled[:most_starts], TOK_DEV)
            return jnp.sort(chosen)
        offsets = jax.vmap(block_offsets)(jax.random.split(key_offsets, block_total), counts)
        offsets = offsets.at[0, 0].set(0)
        starts = jnp.arange(block_total, dtype=jnp.int32)[:, None] * TOK_DEV + offsets
        first_slot = jnp.cumsum(counts) - counts
        target = first_slot[:, None] + jnp.arange(most_starts)[None, :]
        target = jnp.where(offsets < TOK_DEV, target, IMAGES)
        empty = jnp.zeros((IMAGES,), jnp.int32)
        return empty.at[target.reshape(-1)].set(starts.reshape(-1).astype(jnp.int32), mode='drop')
    return jax.vmap(document_positions)(jax.random.split(key, DOCS)).astype(jnp.int32)


def steps_of(key, shape, cuts, smallest, high):
    def one(dim, parts):
        steps = jax.random.uniform(jax.random.fold_in(jax.random.fold_in(key, 6), dim), (parts,), jnp.float32, smallest / len(cuts), high / len(cuts))
        return jnp.repeat(jnp.exp(steps), shape[dim] // parts).reshape((-1,) + (1,) * (len(shape) - dim - 1))

    factor_of = one(*cuts[0])
    for cut in cuts[1:]:
        factor_of = factor_of * one(*cut)
    return factor_of


def noise(stream_key, shape, scale, reach, cuts=(), held_as=jnp.bfloat16):
    array = scale * jax.random.normal(stream_key, shape, jnp.float32)
    if cuts:
        array = array * steps_of(stream_key, shape, cuts, -0.22, 0.18)
    return jnp.clip(array, -reach, reach).astype(held_as)


def setup_inputs(seed: int = 0) -> dict:
    key_list = jax.random.split(jax.random.key(seed), 8)
    queries = draw_queries(jax.random.fold_in(key_list[7], 71), 0)
    latents = draw_latents(jax.random.fold_in(key_list[7], 71), 0)
    k_weight = noise(key_list[2], (DV, HEADS * HD), DV ** -0.5, 0.15625, ((1, 16),))
    v_weight = noise(key_list[3], (DV, HEADS * HD), DV ** -0.5, 0.15625, ((1, 16),))
    d_context = noise(key_list[4], (DOCS, LENGTH, HEADS * HD), 1.0, 6.0, ((0, 8), (1, 16)))
    image_pos = draw_image_pos(jax.random.fold_in(key_list[7], 71), 0)
    image_slot = jax.vmap(lambda own: jax.random.permutation(own, IMAGES))(jax.random.split(key_list[6], DOCS)).reshape((DOCS, IMAGES)).astype(jnp.int32)
    return dict(queries=queries, latents=latents, k_weight=k_weight, v_weight=v_weight, d_context=d_context, image_pos=image_pos, image_slot=image_slot)


EPSILON = 1e-06

def unit_rms(raw_values):
    inverse = lax.rsqrt(lax.optimization_barrier(jnp.mean(raw_values * raw_values, axis=-1, keepdims=True)) + EPSILON)
    return (raw_values * inverse, inverse)

def unit_rms_back(unit_value, inverse, grad_unit):
    return inverse * (grad_unit - unit_value * lax.optimization_barrier(jnp.mean(grad_unit * unit_value, axis=-1, keepdims=True)))

def attend(query_raw, cotangent, local_image, keys_need, values_need):
    score_scale = 1.0 / math.sqrt(HD)
    query_unit, query_inverse = unit_rms(query_raw.astype(jnp.float32))
    query_b = query_unit.astype(jnp.bfloat16)
    select = (local_image[:, None] == jnp.arange(NEED, dtype=jnp.int32)[None, :]).astype(jnp.float32)
    select_b = select.astype(jnp.bfloat16)
    keys_f = keys_need.astype(jnp.float32)
    values_f = values_need.astype(jnp.float32)
    cot_f = cotangent.astype(jnp.float32)
    scores_wide = jnp.einsum('thd,jlhd->thjl', query_b.astype(jnp.float32), keys_f)
    scores = lax.optimization_barrier(jnp.sum(scores_wide * select[:, None, :, None], axis=2)) * score_scale
    exponent = jnp.exp(scores)
    probability = exponent / lax.optimization_barrier(jnp.sum(exponent, axis=-1, keepdims=True))
    probs_b = probability.astype(jnp.bfloat16)
    probs_wide = (probs_b[:, :, None, :] * select_b[:, None, :, None]).astype(jnp.float32)
    context = jnp.einsum('thjl,jlhd->thd', probs_wide, values_f).astype(jnp.bfloat16)
    dprob_wide = jnp.einsum('thd,jlhd->thjl', cot_f, values_f)
    dprob = lax.optimization_barrier(jnp.sum(dprob_wide * select[:, None, :, None], axis=2))
    dscore = probability * (dprob - lax.optimization_barrier(jnp.sum(probability * dprob, axis=-1, keepdims=True))) * score_scale
    dscore_b = dscore.astype(jnp.bfloat16)
    dscore_wide = (dscore_b[:, :, None, :] * select_b[:, None, :, None]).astype(jnp.float32)
    query_cot = jnp.einsum('thjl,jlhd->thd', dscore_wide, keys_f)
    d_queries = unit_rms_back(query_unit, query_inverse, query_cot).astype(jnp.bfloat16)
    key_part = jnp.einsum('thjl,thd->jlhd', dscore_wide, query_b.astype(jnp.float32)).astype(jnp.bfloat16)
    value_part = jnp.einsum('thjl,thd->jlhd', probs_wide, cot_f).astype(jnp.bfloat16)
    return (context, d_queries, key_part, value_part)

def one_document(queries, latents, k_weight, v_weight, d_context, image_pos, image_slot):
    width = HEADS * HD
    lat_img = latents[image_slot]
    flat_img = lat_img.reshape(IMAGES * LATENTS, DV)
    keys_raw = jnp.dot(flat_img, k_weight, preferred_element_type=jnp.float32).reshape(IMAGES, LATENTS, HEADS, HD)
    key_unit, key_inverse = unit_rms(keys_raw)
    keys = key_unit.astype(jnp.bfloat16)
    values = jnp.dot(flat_img, v_weight, preferred_element_type=jnp.float32).astype(jnp.bfloat16)
    values = values.reshape(IMAGES, LATENTS, HEADS, HD)
    positions = jnp.arange(LENGTH, dtype=jnp.int32)
    visible = lax.optimization_barrier(jnp.sum((image_pos[None, :] <= positions[:, None]).astype(jnp.int32), axis=1)) - 1
    block_total = LENGTH // TOK_DEV

    def one_block(block_index):
        block_begin = (block_index * TOK_DEV).astype(jnp.int32)
        query_block = lax.dynamic_slice_in_dim(queries, block_begin, TOK_DEV, 0).reshape(TOK_DEV, HEADS, HD)
        cot_block = lax.dynamic_slice_in_dim(d_context, block_begin, TOK_DEV, 0).reshape(TOK_DEV, HEADS, HD)
        visible_block = lax.dynamic_slice_in_dim(visible, block_begin, TOK_DEV, 0)
        first_image = visible_block[0]
        needed = jnp.minimum(first_image + jnp.arange(NEED, dtype=jnp.int32), IMAGES - 1).astype(jnp.int32)
        results = attend(query_block, cot_block, visible_block - first_image, keys[needed], values[needed])
        return results + (needed,)
    context, d_queries, key_part, value_part, needed = lax.map(one_block, jnp.arange(block_total, dtype=jnp.int32))
    flat_needed = needed.reshape(-1)
    key_cot = jnp.zeros((IMAGES, LATENTS, HEADS, HD), jnp.float32).at[flat_needed].add(key_part.reshape(-1, LATENTS, HEADS, HD).astype(jnp.float32))
    value_cot = jnp.zeros((IMAGES, LATENTS, HEADS, HD), jnp.float32).at[flat_needed].add(value_part.reshape(-1, LATENTS, HEADS, HD).astype(jnp.float32))
    key_grad = unit_rms_back(key_unit, key_inverse, key_cot).astype(jnp.bfloat16).reshape(IMAGES * LATENTS, width)
    value_grad = value_cot.astype(jnp.bfloat16).reshape(IMAGES * LATENTS, width)
    grad_k = jnp.dot(flat_img.T, key_grad, preferred_element_type=jnp.float32)
    grad_v = jnp.dot(flat_img.T, value_grad, preferred_element_type=jnp.float32)
    latent_img = jnp.dot(key_grad, k_weight.T, preferred_element_type=jnp.float32)
    latent_img = latent_img + jnp.dot(value_grad, v_weight.T, preferred_element_type=jnp.float32)
    latent_img = latent_img.reshape(IMAGES, LATENTS, DV)
    latent_grad = jnp.zeros((IMAGES, LATENTS, DV), jnp.float32).at[image_slot].set(latent_img).astype(jnp.bfloat16)
    return (context.reshape(LENGTH, width), d_queries.reshape(LENGTH, width), latent_grad, grad_k, grad_v)

def reference(queries, latents, k_weight, v_weight, d_context, image_pos, image_slot):

    def per_document(arguments):
        return one_document(arguments[0], arguments[1], k_weight, v_weight, arguments[2], arguments[3], arguments[4])
    context, d_queries, d_latents, grads_k, grads_v = lax.map(per_document, (queries, latents, d_context, image_pos, image_slot))
    return (context, d_queries, d_latents, lax.optimization_barrier(jnp.sum(grads_k, axis=0)), lax.optimization_barrier(jnp.sum(grads_v, axis=0)))
```

```python
import math

import jax
import jax.numpy as jnp
from jax import lax
from jax.experimental import pallas as pl
from jax.experimental.pallas import tpu as pltpu
from jax.sharding import PartitionSpec as P

HD = 128
LATENTS = 64
NEED = 3
SIDE = 4
SEQ = 16
ROWS = NEED * LATENTS
EPSILON = 1e-06
SCALE = 1.0 / math.sqrt(HD)
MESH = pl.DeviceIdType.MESH
F32 = jnp.float32
BF16 = jnp.bfloat16

OFFSETS = (
    (0, 0),
    (1, 0),
    (3, 0),
    (0, 1),
    (0, 3),
    (2, 0),
    (0, 2),
    (1, 1),
    (3, 3),
    (1, 3),
    (3, 1),
    (2, 1),
    (1, 2),
    (2, 3),
    (3, 2),
    (2, 2),
)
X_CODE = sum(o[0] << (2 * i) for i, o in enumerate(OFFSETS[1:]))
Y_CODE = sum(o[1] << (2 * i) for i, o in enumerate(OFFSETS[1:]))


def offset_of(step):
    place = 2 * lax.rem(step + SEQ - 1, SEQ)
    return (
        lax.rem(lax.shift_right_logical(jnp.int32(X_CODE), place), SIDE),
        lax.rem(lax.shift_right_logical(jnp.int32(Y_CODE), place), SIDE),
    )


def nt(a, b):
    return lax.dot_general(a, b, (((1,), (1,)), ((), ())), preferred_element_type=F32)


def tn(a, b):
    return lax.dot_general(a, b, (((0,), (0,)), ((), ())), preferred_element_type=F32)


def nn(a, b):
    return lax.dot_general(a, b, (((1,), (0,)), ((), ())), preferred_element_type=F32)


def mean_last(a):
    return jnp.mean(a, axis=-1, keepdims=True)


def attend_half(query, cotangent, keys, values, image):
    raw = query.astype(F32)
    inverse = lax.rsqrt(mean_last(raw * raw) + EPSILON)
    unit = raw * inverse
    unit_b = unit.astype(BF16)
    is0, is1, is2 = image == 0, image == 1, image == 2

    def choose(wide):
        return jnp.where(
            is0, wide[:LATENTS], jnp.where(is1, wide[LATENTS : 2 * LATENTS], wide[2 * LATENTS :])
        )

    def widen(narrow):
        return jnp.concatenate(
            [jnp.where(own, narrow, 0.0).astype(BF16) for own in (is0, is1, is2)], axis=0
        )

    exponent = jnp.exp(choose(nt(keys, unit_b)) * SCALE)
    probs = exponent * (1.0 / jnp.sum(exponent, axis=0, keepdims=True))
    dprob = choose(nt(values, cotangent))
    dscore = probs * (dprob - jnp.sum(probs * dprob, axis=0, keepdims=True)) * SCALE
    probs_wide = widen(probs)
    dscore_wide = widen(dscore)
    context = tn(probs_wide, values)
    query_cot = tn(dscore_wide, keys)
    d_query = inverse * (query_cot - unit * mean_last(query_cot * unit))
    return (
        context.astype(BF16),
        d_query.astype(BF16),
        nn(dscore_wide, unit_b),
        nn(probs_wide, cotangent),
    )


def attention_kernel(
    pos_ref, slot_ref, lat_ref, kw_ref, vw_ref, q_hbm, c_hbm,
    ctx_hbm, dq_hbm, grad_ref, lat_out,
    lat_all, raw_ref, kv_ref, kv_send, kv_recv, g_send, g_recv, run_ref, img_ref,
    q_buf, c_buf, ctx_buf, dq_buf, first_ref, last_ref,
    a_send, a_recv, f_send, f_recv, b_send, b_recv, q_sem, c_sem, ctx_sem, dq_sem, lat_sem,
):
    tokens = q_hbm.shape[0]
    cols = kw_ref.shape[1]
    wide = 2 * cols
    dp = lax.axis_index("dp")
    me = lax.axis_index("seq")
    mx = lax.div(me, SIDE)
    my = lax.rem(me, SIDE)

    def peer(dx, dy):
        return (dp, lax.rem(mx + dx + SIDE, SIDE) * SIDE + lax.rem(my + dy + SIDE, SIDE))

    def owner_of(step):
        dx, dy = offset_of(step)
        return lax.rem(mx - dx + SIDE, SIDE) * SIDE + lax.rem(my - dy + SIDE, SIDE)

    def part(ref, owner):
        return ref.at[:, pl.ds(pl.multiple_of(owner * cols, cols), cols)]

    def q_copy(step):
        return pltpu.make_async_copy(part(q_hbm, owner_of(step)), q_buf.at[step], q_sem.at[step])

    def c_copy(step):
        return pltpu.make_async_copy(part(c_hbm, owner_of(step)), c_buf.at[step], c_sem.at[step])

    def ctx_copy(step):
        return pltpu.make_async_copy(
            ctx_buf.at[step], part(ctx_hbm, owner_of(step)), ctx_sem.at[step]
        )

    def dq_copy(step):
        return pltpu.make_async_copy(dq_buf.at[step], part(dq_hbm, owner_of(step)), dq_sem.at[step])

    barrier = pltpu.get_barrier_semaphore()
    for dx, dy in OFFSETS[1:]:
        pl.semaphore_signal(barrier, inc=1, device_id=peer(dx, dy), device_id_type=MESH)

    half = LATENTS // 2
    lat_all[mx, my] = lat_ref[...]

    def x_first(d):
        src = lat_ref.at[pl.ds(0, half)]
        return pltpu.make_async_remote_copy(
            src_ref=src,
            dst_ref=lat_all.at[mx, my, pl.ds(0, half)],
            send_sem=a_send.at[0, d - 1],
            recv_sem=a_recv.at[0, d - 1],
            device_id=peer(d, 0),
            device_id_type=MESH,
        )

    def y_first(d):
        src = lat_ref.at[pl.ds(half, half)]
        return pltpu.make_async_remote_copy(
            src_ref=src,
            dst_ref=lat_all.at[mx, my, pl.ds(half, half)],
            send_sem=a_send.at[1, d - 1],
            recv_sem=a_recv.at[1, d - 1],
            device_id=peer(0, d),
            device_id_type=MESH,
        )

    def y_second(d):
        block = lat_all.at[:, my, pl.ds(0, half)]
        return pltpu.make_async_remote_copy(
            src_ref=block,
            dst_ref=block,
            send_sem=a_send.at[2, d - 1],
            recv_sem=a_recv.at[2, d - 1],
            device_id=peer(0, d),
            device_id_type=MESH,
        )

    def x_second(d):
        block = lat_all.at[mx, :, pl.ds(half, half)]
        return pltpu.make_async_remote_copy(
            src_ref=block,
            dst_ref=block,
            send_sem=a_send.at[3, d - 1],
            recv_sem=a_recv.at[3, d - 1],
            device_id=peer(d, 0),
            device_id_type=MESH,
        )

    pl.semaphore_wait(barrier, SEQ - 1)
    for d in (1, 3, 2):
        x_first(d).start()
        y_first(d).start()

    def fetch(step, carry):
        q_copy(step).start()
        c_copy(step).start()
        return carry

    lax.fori_loop(0, SEQ, fetch, 0)

    def block_images(block, carry):
        count = jnp.int32(-1)
        for i in range(SEQ):
            count = count + (pos_ref[0, i] <= block * tokens).astype(jnp.int32)
        first_ref[block] = count
        return carry

    lax.fori_loop(0, SEQ, block_images, 0)

    def slot_last(slot, carry):
        image = jnp.int32(0)
        for i in range(SEQ):
            image = image + jnp.where(slot_ref[0, i] == slot, i, 0)
        image = jnp.minimum(image, SEQ - 1)
        after = pos_ref[0, jnp.minimum(image + 1, SEQ - 1)]
        end = jnp.where(image == SEQ - 1, SEQ * tokens, after) - 1
        block = jnp.maximum(lax.div(end, tokens), 0)
        place = jnp.clip(image - first_ref[block], 0, NEED - 1)
        last_ref[slot] = block * NEED + place
        return carry

    lax.fori_loop(0, SEQ, slot_last, 0)

    token = me * tokens + lax.broadcasted_iota(jnp.int32, (1, tokens), 1)
    seen = jnp.zeros((1, tokens), jnp.int32) - 1 - first_ref[me]
    for i in range(SEQ):
        seen = seen + (token >= pos_ref[0, i]).astype(jnp.int32)
    img_ref[...] = seen

    for d in (1, 3, 2):
        x_first(d).wait_recv()
    for d in (1, 3, 2):
        y_second(d).start()
    for d in (1, 3, 2):
        y_first(d).wait_recv()
    for d in (1, 3, 2):
        x_second(d).start()
    for d in (1, 3, 2):
        y_second(d).wait_recv()
        x_second(d).wait_recv()
    lat_copy = pltpu.make_async_copy(lat_all, lat_out, lat_sem)
    lat_copy.start()

    def project(chunk, carry):
        rows = pl.ds(pl.multiple_of(chunk * SIDE * LATENTS, SIDE * LATENTS), SIDE * LATENTS)
        slots = pl.ds(chunk * SIDE, SIDE)
        latents = lat_all[chunk].reshape(SIDE * LATENTS, lat_ref.shape[1])
        raw = nn(latents, kw_ref[...])
        raw_ref[rows, :] = raw
        for head in range(cols // HD):
            one = raw[:, head * HD : (head + 1) * HD]
            unit = one * lax.rsqrt(mean_last(one * one) + EPSILON)
            kv_ref[slots, :, head * HD : (head + 1) * HD] = unit.astype(BF16).reshape(
                SIDE, LATENTS, HD
            )
        values = nn(latents, vw_ref[...]).astype(BF16)
        kv_ref[slots, :, cols:] = values.reshape(SIDE, LATENTS, cols)
        return carry

    lax.fori_loop(0, SIDE, project, 0)

    def forward(step):
        dx, dy = offset_of(step)
        return pltpu.make_async_remote_copy(
            src_ref=kv_send.at[step],
            dst_ref=kv_recv.at[step],
            send_sem=f_send.at[step],
            recv_sem=f_recv.at[step],
            device_id=peer(dx, dy),
            device_id_type=MESH,
        )

    def backward(step):
        return pltpu.make_async_remote_copy(
            src_ref=g_send.at[step],
            dst_ref=g_recv.at[me],
            send_sem=b_send.at[step],
            recv_sem=b_recv.at[me],
            device_id=(dp, owner_of(step)),
            device_id_type=MESH,
        )

    def arrival(block):
        return pltpu.make_async_remote_copy(
            src_ref=g_send.at[0],
            dst_ref=g_recv.at[block],
            send_sem=b_send.at[0],
            recv_sem=b_recv.at[block],
            device_id=(dp, block),
            device_id_type=MESH,
        )

    def needed(block, j):
        slot = slot_ref[0, jnp.minimum(first_ref[block] + j, SEQ - 1)]
        return kv_ref[slot]

    for j in range(NEED):
        kv_recv[0, j * LATENTS : (j + 1) * LATENTS, :] = needed(me, j)

    def send(step, carry):
        dx, dy = offset_of(step)
        block = peer(dx, dy)[1]
        for j in range(NEED):
            kv_send[step, j * LATENTS : (j + 1) * LATENTS, :] = needed(block, j)
        forward(step).start()
        return carry

    lax.fori_loop(1, SEQ, send, 0)

    def attend(step, carry):
        @pl.when(step > 0)
        def _():
            forward(step).wait_recv()

        q_copy(step).wait()
        c_copy(step).wait()
        for head in range(cols // HD):
            lanes = slice(head * HD, (head + 1) * HD)
            lanes_v = slice(cols + head * HD, cols + (head + 1) * HD)
            keys = kv_recv[step, :, lanes]
            values = kv_recv[step, :, lanes_v]
            key_part = jnp.zeros((ROWS, HD), F32)
            value_part = jnp.zeros((ROWS, HD), F32)
            size = 256
            for begin in range(0, tokens, size):
                rows = slice(begin, begin + size)
                context, d_query, key_add, value_add = attend_half(
                    q_buf[step, rows, lanes],
                    c_buf[step, rows, lanes],
                    keys,
                    values,
                    img_ref[:, rows],
                )
                ctx_buf[step, rows, lanes] = context
                dq_buf[step, rows, lanes] = d_query
                key_part = key_part + key_add
                value_part = value_part + value_add
            g_send[step, :, lanes] = key_part.astype(BF16)
            g_send[step, :, lanes_v] = value_part.astype(BF16)

        ctx_copy(step).start()
        dq_copy(step).start()

        @pl.when(step > 0)
        def _():
            backward(step).start()

        @pl.when(step == 0)
        def _():
            g_recv[me] = g_send[0]

        return carry

    lax.fori_loop(0, SEQ, attend, 0)

    def combine(block, run):
        @pl.when(block != me)
        def _():
            arrival(block).wait_recv()

        first = first_ref[block]
        end = (block + 1) * tokens - 1
        before = block * tokens - 1
        last = jnp.int32(-1)
        previous = jnp.int32(-1)
        for i in range(SEQ):
            last = last + (pos_ref[0, i] <= end).astype(jnp.int32)
            previous = previous + (pos_ref[0, i] <= before).astype(jnp.int32)
        for j in range(NEED):
            same = previous == first if j == 0 else first + j > last
            keep = jnp.where(same, 1.0, 0.0).astype(F32)
            run = run * keep + g_recv[block, j * LATENTS : (j + 1) * LATENTS, :].astype(F32)
            run_ref[block * NEED + j] = run
        return run

    lax.fori_loop(0, SEQ, combine, jnp.zeros((LATENTS, wide), F32))

    def key_grads(slot, carry):
        rows = pl.ds(pl.multiple_of(slot * LATENTS, LATENTS), LATENTS)
        total = run_ref[last_ref[slot]]
        for head in range(cols // HD):
            lanes = slice(head * HD, (head + 1) * HD)
            raw = raw_ref[rows, lanes]
            cot = total[:, lanes]
            inverse = lax.rsqrt(mean_last(raw * raw) + EPSILON)
            unit = raw * inverse
            grad_ref[rows, lanes] = (inverse * (cot - unit * mean_last(cot * unit))).astype(BF16)
        grad_ref[rows, cols:] = total[:, cols:].astype(BF16)
        return carry

    lax.fori_loop(0, SEQ, key_grads, 0)

    for d in (1, 2, 3):
        x_first(d).wait_send()
        y_first(d).wait_send()
        y_second(d).wait_send()
        x_second(d).wait_send()
    lat_copy.wait()

    def drain(step, carry):
        @pl.when(step > 0)
        def _():
            forward(step).wait_send()
            backward(step).wait_send()

        ctx_copy(step).wait()
        dq_copy(step).wait()
        return carry

    lax.fori_loop(0, SEQ, drain, 0)


def attention_call(positions, slots, latents, k_weight, v_weight, queries, cotangents):
    tokens, width = queries.shape
    cols = k_weight.shape[1]
    model = latents.shape[1]
    wide = 2 * cols
    smem = pl.BlockSpec(memory_space=pltpu.SMEM)
    vmem = pl.BlockSpec(memory_space=pltpu.VMEM)
    hbm = pl.BlockSpec(memory_space=pl.ANY)
    dma = pltpu.SemaphoreType.DMA
    return pl.pallas_call(
        attention_kernel,
        name="attention",
        out_shape=(
            jax.ShapeDtypeStruct((tokens, width), BF16),
            jax.ShapeDtypeStruct((tokens, width), BF16),
            jax.ShapeDtypeStruct((SEQ * LATENTS, wide), BF16),
            jax.ShapeDtypeStruct((SIDE, SIDE, LATENTS, model), BF16),
        ),
        in_specs=[smem, smem, vmem, vmem, vmem, hbm, hbm],
        out_specs=(hbm, hbm, vmem, hbm),
        scratch_shapes=[
            pltpu.VMEM((SIDE, SIDE, LATENTS, model), BF16),
            pltpu.VMEM((SEQ * LATENTS, cols), F32),
            pltpu.VMEM((SEQ, LATENTS, wide), BF16),
            pltpu.VMEM((SEQ, ROWS, wide), BF16),
            pltpu.VMEM((SEQ, ROWS, wide), BF16),
            pltpu.VMEM((SEQ, ROWS, wide), BF16),
            pltpu.VMEM((SEQ, ROWS, wide), BF16),
            pltpu.VMEM((SEQ * NEED, LATENTS, wide), F32),
            pltpu.VMEM((1, tokens), jnp.int32),
            pltpu.VMEM((SEQ, tokens, cols), BF16),
            pltpu.VMEM((SEQ, tokens, cols), BF16),
            pltpu.VMEM((SEQ, tokens, cols), BF16),
            pltpu.VMEM((SEQ, tokens, cols), BF16),
            pltpu.SMEM((SEQ,), jnp.int32),
            pltpu.SMEM((SEQ,), jnp.int32),
            dma((4, SIDE - 1)),
            dma((4, SIDE - 1)),
            dma((SEQ,)),
            dma((SEQ,)),
            dma((SEQ,)),
            dma((SEQ,)),
            dma((SEQ,)),
            dma((SEQ,)),
            dma((SEQ,)),
            dma((SEQ,)),
            dma(()),
        ],
        compiler_params=pltpu.CompilerParams(
            collective_id=0, has_side_effects=True, vmem_limit_bytes=56 * 2**20
        ),
    )(positions, slots, latents, k_weight, v_weight, queries, cotangents)


def gradient_kernel(
    grad_ref, lat_ref, kw_ref, vw_ref,
    dlat_ref, dw_ref,
    dw_send, core_recv, z_send, z_recv, final_ref, da_send, db_send, da_recv, db_recv, ea_send, eb_send, ea_recv, eb_recv,
    core_ss, core_rs, z_ss, z_rs, g_ss, g_rs, h_ss, h_rs, a_ss, a_rs, b_ss, b_rs, ea_ss, ea_rs, eb_ss, eb_rs,
):
    model = kw_ref.shape[0]
    cols = kw_ref.shape[1]
    half = model // 2
    piece = half // SIDE
    dp = lax.axis_index("dp")
    me = lax.axis_index("seq")
    mx = lax.div(me, SIDE)
    my = lax.rem(me, SIDE)
    mz = lax.div(dp, 2)
    core = lax.rem(dp, 2)

    def ring(base, d):
        return lax.rem(base + d, SIDE)

    def x_peer(d):
        return (dp, ring(mx, d) * SIDE + my)

    def y_peer(d):
        return (dp, mx * SIDE + ring(my, d))

    def z_peer(d):
        return (ring(mz, d) * 2 + core, me)

    core_peer = (mz * 2 + 1 - core, me)

    def remote(src, dst, send_sem, recv_sem, device):
        return pltpu.make_async_remote_copy(
            src_ref=src,
            dst_ref=dst,
            send_sem=send_sem,
            recv_sem=recv_sem,
            device_id=device,
            device_id_type=MESH,
        )

    barrier = pltpu.get_barrier_semaphore()
    for d in (1, 2, 3):
        for device in (x_peer(d), y_peer(d), z_peer(d)):
            pl.semaphore_signal(barrier, inc=1, device_id=device, device_id_type=MESH)
    pl.semaphore_signal(barrier, inc=1, device_id=core_peer, device_id_type=MESH)

    chunk = 128

    def weight_grad(base):
        def one(i, carry):
            rows = pl.ds(pl.multiple_of(base + i * chunk, chunk), chunk)
            dw_send[rows, :] = tn(lat_ref[:, rows], grad_ref[...]).astype(BF16)
            return carry

        lax.fori_loop(0, half // chunk, one, 0)

    own_rows = pl.multiple_of(core * half, half)
    other_rows = pl.multiple_of((1 - core) * half, half)
    core_copy = remote(
        dw_send.at[pl.ds(other_rows, half)], core_recv, core_ss, core_rs, core_peer
    )

    def da_copy(d):
        return remote(
            da_send.at[ring(mx, d)], da_recv.at[d - 1], a_ss.at[d - 1], a_rs.at[d - 1], x_peer(d)
        )

    def db_copy(d):
        return remote(
            db_send.at[:, ring(my, d)], db_recv.at[d - 1], b_ss.at[d - 1], b_rs.at[d - 1], y_peer(d)
        )

    def ea_copy(d):
        return remote(
            ea_send.at[ring(my, d)], ea_recv.at[d - 1], ea_ss.at[d - 1], ea_rs.at[d - 1], y_peer(d)
        )

    def eb_copy(d):
        return remote(
            eb_send.at[ring(mx, d)], eb_recv.at[d - 1], eb_ss.at[d - 1], eb_rs.at[d - 1], x_peer(d)
        )

    def z_copy(d):
        rows = pl.ds(pl.multiple_of(ring(mz, d) * piece, 32), piece)
        return remote(z_send.at[rows], z_recv.at[d - 1], z_ss.at[d - 1], z_rs.at[d - 1], z_peer(d))

    def final_rows(z, c):
        return pl.ds(pl.multiple_of(c * half + z * piece, 32), piece)

    def g_copy(d):
        block = final_ref.at[final_rows(mz, core)]
        return remote(block, block, g_ss.at[d - 1], g_rs.at[d - 1], z_peer(d))

    def h_copy(d):
        block = final_ref.at[final_rows(ring(mz, SIDE - d), core)]
        return remote(block, block, h_ss.at[d], h_rs.at[d], core_peer)

    weight_grad(other_rows)
    pl.semaphore_wait(barrier, 3 * (SIDE - 1) + 1)
    core_copy.start()

    def latent_grad(x):
        rows = pl.ds(pl.multiple_of(x * SIDE * LATENTS, SIDE * LATENTS), SIDE * LATENTS)
        keys = grad_ref[rows, :cols]
        values = grad_ref[rows, cols:]
        shape = (SIDE, LATENTS, half)
        da_send[x] = (
            (nt(keys, kw_ref[:half]) + nt(values, vw_ref[:half])).astype(BF16).reshape(shape)
        )
        db_send[x] = (
            (nt(keys, kw_ref[half:]) + nt(values, vw_ref[half:])).astype(BF16).reshape(shape)
        )

    def latent_grads(d, carry):
        latent_grad(ring(mx, d))

        @pl.when(d > 0)
        def _():
            da_copy(d).start()

        return carry

    lax.fori_loop(0, SIDE, latent_grads, 0)
    for d in (1, 3, 2):
        db_copy(d).start()

    weight_grad(own_rows)
    core_copy.wait_recv()

    def core_sum(i, carry):
        rows = pl.ds(pl.multiple_of(i * piece, 32), piece)
        own = pl.ds(pl.multiple_of(own_rows + i * piece, 32), piece)
        z_send[rows, :] = (dw_send[own, :].astype(F32) + core_recv[rows, :].astype(F32)).astype(
            BF16
        )
        return carry

    lax.fori_loop(0, SIDE, core_sum, 0)
    for d in (1, 3, 2):
        z_copy(d).start()

    for d in (1, 2, 3):
        da_copy(d).wait_recv()

    def sum_a(y, carry):
        total = da_send[mx, y].astype(F32)
        for d in range(SIDE - 1):
            total = total + da_recv[d, y].astype(F32)
        ea_send[y] = total.astype(BF16)
        return carry

    lax.fori_loop(0, SIDE, sum_a, 0)
    for d in (1, 3, 2):
        ea_copy(d).start()
    for d in (1, 2, 3):
        db_copy(d).wait_recv()

    def sum_b(x, carry):
        total = db_send[x, my].astype(F32)
        for d in range(SIDE - 1):
            total = total + db_recv[d, x].astype(F32)
        eb_send[x] = total.astype(BF16)
        return carry

    lax.fori_loop(0, SIDE, sum_b, 0)
    for d in (1, 3, 2):
        eb_copy(d).start()

    for d in (1, 2, 3):
        z_copy(d).wait_recv()
    own_piece = pl.ds(pl.multiple_of(mz * piece, 32), piece)
    total = z_send[own_piece, :].astype(F32)
    for d in range(SIDE - 1):
        total = total + z_recv[d].astype(F32)
    final_ref[final_rows(mz, core), :] = total.astype(BF16)
    for d in (1, 3, 2):
        g_copy(d).start()
    h_copy(0).start()

    for d in (1, 2, 3):
        ea_copy(d).wait_recv()
    total = ea_send[my].astype(F32)
    for d in range(SIDE - 1):
        total = total + ea_recv[d].astype(F32)
    dlat_ref[:, :half] = total.astype(BF16)
    for d in (1, 2, 3):
        eb_copy(d).wait_recv()
    total = eb_send[mx].astype(F32)
    for d in range(SIDE - 1):
        total = total + eb_recv[d].astype(F32)
    dlat_ref[:, half:] = total.astype(BF16)

    for d in (1, 3, 2):
        g_copy(d).wait_recv()
        h_copy(d).start()
    for d in range(SIDE):
        h_copy(d).wait_recv()

    def write(i, carry):
        rows = pl.ds(pl.multiple_of(i * piece, 32), piece)
        dw_ref[rows, :] = final_ref[rows, :]
        return carry

    lax.fori_loop(0, 2 * SIDE, write, 0)

    core_copy.wait_send()
    for d in (1, 2, 3):
        for copy in (da_copy(d), db_copy(d), ea_copy(d), eb_copy(d), z_copy(d), g_copy(d)):
            copy.wait_send()
    for d in range(SIDE):
        h_copy(d).wait_send()


def gradient_call(grads, latents, k_weight, v_weight):
    model, cols = k_weight.shape
    half = model // 2
    piece = half // SIDE
    wide = 2 * cols
    vmem = pl.BlockSpec(memory_space=pltpu.VMEM)
    dma = pltpu.SemaphoreType.DMA
    peers = SIDE - 1
    return pl.pallas_call(
        gradient_kernel,
        name="gradients",
        out_shape=(
            jax.ShapeDtypeStruct((LATENTS, model), BF16),
            jax.ShapeDtypeStruct((model, wide), BF16),
        ),
        in_specs=[vmem] * 4,
        out_specs=(vmem, vmem),
        scratch_shapes=[
            pltpu.VMEM((model, wide), BF16),
            pltpu.VMEM((half, wide), BF16),
            pltpu.VMEM((half, wide), BF16),
            pltpu.VMEM((peers, piece, wide), BF16),
            pltpu.VMEM((model, wide), BF16),
            pltpu.VMEM((SIDE, SIDE, LATENTS, half), BF16),
            pltpu.VMEM((SIDE, SIDE, LATENTS, half), BF16),
            pltpu.VMEM((peers, SIDE, LATENTS, half), BF16),
            pltpu.VMEM((peers, SIDE, LATENTS, half), BF16),
            pltpu.VMEM((SIDE, LATENTS, half), BF16),
            pltpu.VMEM((SIDE, LATENTS, half), BF16),
            pltpu.VMEM((peers, LATENTS, half), BF16),
            pltpu.VMEM((peers, LATENTS, half), BF16),
            dma(()),
            dma(()),
            dma((peers,)),
            dma((peers,)),
            dma((peers,)),
            dma((peers,)),
            dma((SIDE,)),
            dma((SIDE,)),
        ]
        + [dma((peers,))] * 8,
        compiler_params=pltpu.CompilerParams(
            collective_id=1, has_side_effects=True, vmem_limit_bytes=56 * 2**20
        ),
    )(grads, latents, k_weight, v_weight)


def local(queries, latents, k_weight, v_weight, d_context, image_pos, image_slot):
    model, cols = k_weight.shape
    context, d_queries, grads, lat_all = attention_call(
        image_pos, image_slot, latents[0, 0], k_weight, v_weight, queries[0], d_context[0]
    )
    d_latents, d_weights = gradient_call(
        grads, lat_all.reshape(SEQ * LATENTS, model), k_weight, v_weight
    )
    d_weights = d_weights.astype(F32)
    return (
        context[None],
        d_queries[None],
        d_latents[None, None],
        d_weights[:, :cols],
        d_weights[:, cols:],
    )


def solution(mesh):
    in_specs = (
        P("dp", "seq", None),
        P("dp", "seq", None, None),
        P(None, "seq"),
        P(None, "seq"),
        P("dp", "seq", None),
        P("dp", None),
        P("dp", None),
    )
    out_specs = (
        P("dp", "seq", None),
        P("dp", "seq", None),
        P("dp", "seq", None, None),
        P(None, "seq"),
        P(None, "seq"),
    )
    return jax.shard_map(local, mesh=mesh, in_specs=in_specs, out_specs=out_specs, check_vma=False)
```

```python
import math

import jax
import jax.numpy as jnp
from jax import lax
from jax.experimental import pallas as pl
from jax.experimental.pallas import tpu as pltpu
from jax.sharding import PartitionSpec as P

HD = 128
LATENTS = 64
NEED = 3
SIDE = 4
SEQ = 16
ROWS = NEED * LATENTS
EPSILON = 1e-06
SCALE = 1.0 / math.sqrt(HD)
MESH = pl.DeviceIdType.MESH
F32 = jnp.float32
BF16 = jnp.bfloat16

OFFSETS = (
    (0, 0),
    (1, 0),
    (3, 0),
    (0, 1),
    (0, 3),
    (2, 0),
    (0, 2),
    (1, 1),
    (3, 3),
    (1, 3),
    (3, 1),
    (2, 1),
    (1, 2),
    (2, 3),
    (3, 2),
    (2, 2),
)
X_CODE = sum(o[0] << (2 * i) for i, o in enumerate(OFFSETS[1:]))
Y_CODE = sum(o[1] << (2 * i) for i, o in enumerate(OFFSETS[1:]))


def offset_of(step):
    place = 2 * lax.rem(step + SEQ - 1, SEQ)
    return (
        lax.rem(lax.shift_right_logical(jnp.int32(X_CODE), place), SIDE),
        lax.rem(lax.shift_right_logical(jnp.int32(Y_CODE), place), SIDE),
    )


def nt(a, b):
    return lax.dot_general(a, b, (((1,), (1,)), ((), ())), preferred_element_type=F32)


def tn(a, b):
    return lax.dot_general(a, b, (((0,), (0,)), ((), ())), preferred_element_type=F32)


def nn(a, b):
    return lax.dot_general(a, b, (((1,), (0,)), ((), ())), preferred_element_type=F32)


def mean_last(a):
    return jnp.mean(a, axis=-1, keepdims=True)


def attend_half(query, cotangent, keys, values, image):
    raw = query.astype(F32)
    inverse = lax.rsqrt(mean_last(raw * raw) + EPSILON)
    unit = raw * inverse
    unit_b = unit.astype(BF16)
    is0, is1, is2 = image == 0, image == 1, image == 2

    def choose(wide):
        return jnp.where(
            is0, wide[:LATENTS], jnp.where(is1, wide[LATENTS : 2 * LATENTS], wide[2 * LATENTS :])
        )

    def widen(narrow):
        return jnp.concatenate(
            [jnp.where(own, narrow, 0.0).astype(BF16) for own in (is0, is1, is2)], axis=0
        )

    exponent = jnp.exp(choose(nt(keys, unit_b)) * SCALE)
    probs = exponent * (1.0 / jnp.sum(exponent, axis=0, keepdims=True))
    dprob = choose(nt(values, cotangent))
    dscore = probs * (dprob - jnp.sum(probs * dprob, axis=0, keepdims=True)) * SCALE
    probs_wide = widen(probs)
    dscore_wide = widen(dscore)
    context = tn(probs_wide, values)
    query_cot = tn(dscore_wide, keys)
    d_query = inverse * (query_cot - unit * mean_last(query_cot * unit))
    return (
        context.astype(BF16),
        d_query.astype(BF16),
        nn(dscore_wide, unit_b),
        nn(probs_wide, cotangent),
    )


def whole_kernel(
    pos_ref, slot_ref, lat_ref, kw_ref, vw_ref, q_hbm, c_hbm,
    ctx_hbm, dq_hbm, dlat_ref, dk_hbm, dv_hbm,
    lat_all, lat_t, w_ref, w_t, unit_ref, inv_ref, kv_ref, kv_send, kv_recv, g_send, g_recv, run_ref, grad_ref, img_ref,
    q_buf, c_buf, first_ref, last_ref, keep_ref,
    dw_send, core_recv, z_send, z_recv, final_ref,
    da_send, db_send, da_recv, db_recv, ea_send, eb_send, ea_recv, eb_recv,
    l_ss, l_rs, f_ss, f_rs, b_ss, b_rs, q_sem, c_sem, ctx_sem, dq_sem,
    core_ss, core_rs, z_ss, z_rs, g_ss, g_rs, h_ss, h_rs, d_ss, d_rs, out_sem,
):
    tokens = q_hbm.shape[0]
    model = lat_ref.shape[1]
    cols = kw_ref.shape[1]
    heads = cols // HD
    pair = 2 * HD
    half = model // 2
    piece = half // SIDE
    group = SIDE * LATENTS
    peers = (1, 3, 2)
    dp = lax.axis_index("dp")
    me = lax.axis_index("seq")
    mx = lax.div(me, SIDE)
    my = lax.rem(me, SIDE)
    mz = lax.div(dp, 2)
    core = lax.rem(dp, 2)

    def ring(base, d):
        return lax.rem(base + d, SIDE)

    def peer(dx, dy):
        return (dp, ring(mx, dx) * SIDE + ring(my, dy))

    def z_peer(d):
        return (ring(mz, d) * 2 + core, me)

    core_peer = (mz * 2 + 1 - core, me)

    def owner_of(step):
        dx, dy = offset_of(step)
        return ring(mx, SIDE - dx) * SIDE + ring(my, SIDE - dy)

    def remote(src, dst, send_sem, recv_sem, device):
        return pltpu.make_async_remote_copy(
            src_ref=src,
            dst_ref=dst,
            send_sem=send_sem,
            recv_sem=recv_sem,
            device_id=device,
            device_id_type=MESH,
        )

    def lanes_of(n):
        place = owner_of(lax.rem(n, SEQ)) * cols + lax.div(n, SEQ) * HD
        return pl.ds(pl.multiple_of(place, HD), HD)

    def q_copy(n):
        return pltpu.make_async_copy(q_hbm.at[:, lanes_of(n)], q_buf.at[n], q_sem.at[n])

    def c_copy(n):
        return pltpu.make_async_copy(c_hbm.at[:, lanes_of(n)], c_buf.at[n], c_sem.at[n])

    def ctx_copy(n):
        return pltpu.make_async_copy(c_buf.at[n], ctx_hbm.at[:, lanes_of(n)], ctx_sem.at[n])

    def dq_copy(n):
        return pltpu.make_async_copy(q_buf.at[n], dq_hbm.at[:, lanes_of(n)], dq_sem.at[n])

    barrier = pltpu.get_barrier_semaphore()
    for dx, dy in OFFSETS[1:]:
        pl.semaphore_signal(barrier, inc=1, device_id=peer(dx, dy), device_id_type=MESH)
    for d in peers:
        pl.semaphore_signal(barrier, inc=1, device_id=z_peer(d), device_id_type=MESH)
    pl.semaphore_signal(barrier, inc=1, device_id=core_peer, device_id_type=MESH)

    low = pl.ds(0, LATENTS // 2)
    high = pl.ds(LATENTS // 2, LATENTS // 2)

    def x_first(d):
        return remote(
            lat_ref.at[low], lat_all.at[mx, my, low], l_ss.at[0, d], l_rs.at[0, d], peer(d, 0)
        )

    def y_first(d):
        return remote(
            lat_ref.at[high], lat_all.at[mx, my, high], l_ss.at[1, d], l_rs.at[1, d], peer(0, d)
        )

    def y_second(d):
        block = lat_all.at[:, my, low]
        return remote(block, block, l_ss.at[2, d], l_rs.at[2, d], peer(0, d))

    def x_second(d):
        block = lat_all.at[mx, :, high]
        return remote(block, block, l_ss.at[3, d], l_rs.at[3, d], peer(d, 0))

    lat_all[mx, my] = lat_ref[...]
    pl.semaphore_wait(barrier, SEQ - 1 + SIDE)
    for d in peers:
        x_first(d).start()
        y_first(d).start()

    def fetch(n, carry):
        q_copy(n).start()
        c_copy(n).start()
        return carry

    lax.fori_loop(0, heads * SEQ, fetch, 0)

    for head in range(heads):
        lanes = slice(head * HD, (head + 1) * HD)
        w_ref[:, head * pair : head * pair + HD] = kw_ref[:, lanes]
        w_ref[:, head * pair + HD : (head + 1) * pair] = vw_ref[:, lanes]

    def block_images(block, carry):
        count = jnp.int32(-1)
        for i in range(SEQ):
            count = count + (pos_ref[0, i] <= block * tokens).astype(jnp.int32)
        first_ref[block] = count
        return carry

    lax.fori_loop(0, SEQ, block_images, 0)

    def slot_last(slot, carry):
        image = jnp.int32(0)
        for i in range(SEQ):
            image = image + jnp.where(slot_ref[0, i] == slot, i, 0)
        image = jnp.minimum(image, SEQ - 1)
        after = pos_ref[0, jnp.minimum(image + 1, SEQ - 1)]
        end = jnp.where(image == SEQ - 1, SEQ * tokens, after) - 1
        block = jnp.maximum(lax.div(end, tokens), 0)
        place = jnp.clip(image - first_ref[block], 0, NEED - 1)
        last_ref[slot] = block * NEED + place
        return carry

    lax.fori_loop(0, SEQ, slot_last, 0)

    token = me * tokens + lax.broadcasted_iota(jnp.int32, (1, tokens), 1)
    seen = jnp.zeros((1, tokens), jnp.int32) - 1 - first_ref[me]
    for i in range(SEQ):
        seen = seen + (token >= pos_ref[0, i]).astype(jnp.int32)
    img_ref[...] = seen

    for d in peers:
        x_first(d).wait_recv()
    for d in peers:
        y_second(d).start()
    for d in peers:
        y_first(d).wait_recv()
    for d in peers:
        x_second(d).start()
    for d in peers:
        y_second(d).wait_recv()
        x_second(d).wait_recv()

    def project(x, carry):
        rows = pl.ds(pl.multiple_of(x * group, group), group)
        slots = pl.ds(x * SIDE, SIDE)
        raw = nn(lat_all[x].reshape(group, model), w_ref[...])
        for head in range(heads):
            one = raw[:, head * pair : head * pair + HD]
            inverse = lax.rsqrt(mean_last(one * one) + EPSILON)
            unit = one * inverse
            unit_ref[head, rows, :] = unit
            inv_ref[head, rows, :] = jnp.broadcast_to(inverse, unit.shape)
            kv_ref[slots, :, head * pair : head * pair + HD] = unit.astype(BF16).reshape(
                SIDE, LATENTS, HD
            )
            values = raw[:, head * pair + HD : (head + 1) * pair].astype(BF16)
            kv_ref[slots, :, head * pair + HD : (head + 1) * pair] = values.reshape(
                SIDE, LATENTS, HD
            )
        return carry

    lax.fori_loop(0, SIDE, project, 0)

    def forward(n):
        dx, dy = offset_of(lax.rem(n, SEQ))
        return remote(kv_send.at[n], kv_recv.at[n], f_ss.at[n], f_rs.at[n], peer(dx, dy))

    def backward(n):
        place = lax.div(n, SEQ) * SEQ + me
        return remote(
            g_send.at[n],
            g_recv.at[place],
            b_ss.at[n],
            b_rs.at[place],
            (dp, owner_of(lax.rem(n, SEQ))),
        )

    def arrival(n):
        return remote(g_send.at[0], g_recv.at[n], b_ss.at[0], b_rs.at[n], (dp, lax.rem(n, SEQ)))

    def prepare(target, n, head, block):
        for j in range(NEED):
            slot = slot_ref[0, jnp.minimum(first_ref[block] + j, SEQ - 1)]
            both = kv_ref[slot]
            target[n, j * LATENTS : (j + 1) * LATENTS, :] = both[:, head * pair : (head + 1) * pair]

    for head in range(heads):

        def send(step, carry, head=head):
            n = head * SEQ + step
            dx, dy = offset_of(step)
            prepare(kv_send, n, head, peer(dx, dy)[1])
            forward(n).start()
            return carry

        lax.fori_loop(1, SEQ, send, 0)
    for head in range(heads):
        prepare(kv_recv, head * SEQ, head, me)

    def turn(x, carry):
        rows = pl.ds(pl.multiple_of(x * group, group), group)
        lat_t[:, rows] = lat_all[x].reshape(group, model).T
        return carry

    lax.fori_loop(0, SIDE, turn, 0)
    w_t[...] = w_ref[...].T

    def keep_flags(block, carry):
        first = first_ref[block]
        end = (block + 1) * tokens - 1
        before = block * tokens - 1
        last = jnp.int32(-1)
        previous = jnp.int32(-1)
        for i in range(SEQ):
            last = last + (pos_ref[0, i] <= end).astype(jnp.int32)
            previous = previous + (pos_ref[0, i] <= before).astype(jnp.int32)
        for j in range(NEED):
            same = previous == first if j == 0 else first + j > last
            keep_ref[block * NEED + j] = same.astype(jnp.int32)
        return carry

    lax.fori_loop(0, SEQ, keep_flags, 0)

    def attend(n, carry):
        own = lax.rem(n, SEQ) == 0

        @pl.when(jnp.logical_not(own))
        def _():
            forward(n).wait_recv()

        q_copy(n).wait()
        c_copy(n).wait()
        keys = kv_recv[n, :, :HD]
        values = kv_recv[n, :, HD:]
        key_part = jnp.zeros((ROWS, HD), F32)
        value_part = jnp.zeros((ROWS, HD), F32)
        size = 256
        for begin in range(0, tokens, size):
            rows = slice(begin, begin + size)
            context, d_query, key_add, value_add = attend_half(
                q_buf[n, rows, :], c_buf[n, rows, :], keys, values, img_ref[:, rows]
            )
            c_buf[n, rows, :] = context
            q_buf[n, rows, :] = d_query
            key_part = key_part + key_add
            value_part = value_part + value_add
        g_send[n, :, :HD] = key_part.astype(BF16)
        g_send[n, :, HD:] = value_part.astype(BF16)

        @pl.when(jnp.logical_not(own))
        def _():
            backward(n).start()

        @pl.when(own)
        def _():
            g_recv[lax.div(n, SEQ) * SEQ + me] = g_send[n]

        ctx_copy(n).start()
        dq_copy(n).start()
        return carry

    lax.fori_loop(0, heads * SEQ, attend, 0)

    def key_value_grads(head):
        def combine(block, run):
            @pl.when(block != me)
            def _():
                arrival(head * SEQ + block).wait_recv()

            for j in range(NEED):
                keep = keep_ref[block * NEED + j].astype(F32)
                part = g_recv[head * SEQ + block, j * LATENTS : (j + 1) * LATENTS, :]
                run = run * keep + part.astype(F32)
                run_ref[block * NEED + j] = run
            return run

        lax.fori_loop(0, SEQ, combine, jnp.zeros((LATENTS, pair), F32))

        def finish(x, carry):
            rows = pl.ds(pl.multiple_of(x * group, group), group)
            total = jnp.concatenate([run_ref[last_ref[x * SIDE + y]] for y in range(SIDE)], axis=0)
            cot = total[:, :HD]
            unit = unit_ref[head, rows, :]
            key_grad = inv_ref[head, rows, :] * (cot - unit * mean_last(cot * unit))
            shape = (SIDE, LATENTS, HD)
            lanes = slice(head * pair, head * pair + HD)
            grad_ref[x, :, :, lanes] = key_grad.astype(BF16).reshape(shape)
            lanes = slice(head * pair + HD, (head + 1) * pair)
            grad_ref[x, :, :, lanes] = total[:, HD:].astype(BF16).reshape(shape)
            return carry

        lax.fori_loop(0, SIDE, finish, 0)

    own_rows = pl.multiple_of(core * half, half)
    other_rows = pl.multiple_of((1 - core) * half, half)

    def weight_grad(head, base):
        chunk = half // 2

        def one(i, carry):
            rows = pl.ds(pl.multiple_of(base + i * chunk, chunk), chunk)
            grads = grad_ref[:, :, :, head * pair : (head + 1) * pair]
            grads = grads.reshape(SEQ * LATENTS, pair)
            dw_send[head, rows, :] = nn(lat_t[rows, :], grads).astype(BF16)
            return carry

        lax.fori_loop(0, half // chunk, one, 0)

    def core_copy(head):
        return remote(
            dw_send.at[head, pl.ds(other_rows, half)],
            core_recv.at[head],
            core_ss.at[head],
            core_rs.at[head],
            core_peer,
        )

    def z_copy(head, d):
        rows = pl.ds(pl.multiple_of(ring(mz, d) * piece, piece), piece)
        return remote(
            z_send.at[head, rows],
            z_recv.at[head, d - 1],
            z_ss.at[head, d],
            z_rs.at[head, d],
            z_peer(d),
        )

    def final_rows(z, c):
        return pl.ds(pl.multiple_of(c * half + z * piece, piece), piece)

    def g_copy(head, d):
        block = final_ref.at[head, final_rows(mz, core)]
        return remote(block, block, g_ss.at[head, d], g_rs.at[head, d], z_peer(d))

    def h_copy(head, d):
        block = final_ref.at[head, final_rows(ring(mz, SIDE - d), core)]
        return remote(block, block, h_ss.at[head, d], h_rs.at[head, d], core_peer)

    def core_sum(head):
        core_copy(head).wait_recv()

        def one(i, carry):
            rows = pl.ds(pl.multiple_of(i * piece, piece), piece)
            own = pl.ds(pl.multiple_of(own_rows + i * piece, piece), piece)
            total = dw_send[head, own, :].astype(F32) + core_recv[head, rows, :].astype(F32)
            z_send[head, rows, :] = total.astype(BF16)
            return carry

        lax.fori_loop(0, SIDE, one, 0)
        for d in peers:
            z_copy(head, d).start()

    def z_sum(head):
        for d in peers:
            z_copy(head, d).wait_recv()
        total = z_send[head, pl.ds(pl.multiple_of(mz * piece, piece), piece), :].astype(F32)
        for d in peers:
            total = total + z_recv[head, d - 1].astype(F32)
        final_ref[head, final_rows(mz, core), :] = total.astype(BF16)
        for d in peers:
            g_copy(head, d).start()
        h_copy(head, 0).start()

    def hand_over(head):
        for d in peers:
            g_copy(head, d).wait_recv()
            h_copy(head, d).start()

    def out_copy(head, i):
        lanes = pl.ds(head * HD, HD)
        return pltpu.make_async_copy(
            final_ref.at[head, :, pl.ds(i * HD, HD)],
            (dk_hbm, dv_hbm)[i].at[:, lanes],
            out_sem.at[head, i],
        )

    def weight_out(head):
        for d in range(SIDE):
            h_copy(head, d).wait_recv()
        for i in range(2):
            out_copy(head, i).start()

    def da_copy(d):
        return remote(
            da_send.at[ring(mx, d)], da_recv.at[d - 1], d_ss.at[0, d], d_rs.at[0, d], peer(d, 0)
        )

    def db_copy(d):
        return remote(
            db_send.at[ring(my, d)], db_recv.at[d - 1], d_ss.at[1, d], d_rs.at[1, d], peer(0, d)
        )

    def ea_copy(d):
        return remote(
            ea_send.at[ring(my, d)], ea_recv.at[d - 1], d_ss.at[2, d], d_rs.at[2, d], peer(0, d)
        )

    def eb_copy(d):
        return remote(
            eb_send.at[ring(mx, d)], eb_recv.at[d - 1], d_ss.at[3, d], d_rs.at[3, d], peer(d, 0)
        )

    def latent_grads(i, carry):
        d = lax.rem(i + 1, SIDE)
        x = ring(mx, d)
        y = ring(my, d)
        shape = (SIDE, LATENTS, half)
        grads = grad_ref[x].reshape(group, heads * pair)
        da_send[x] = nn(grads, w_t[:, :half]).astype(BF16).reshape(shape)

        @pl.when(d > 0)
        def _():
            da_copy(d).start()

        grads = grad_ref[:, y].reshape(group, heads * pair)
        db_send[y] = nn(grads, w_t[:, half:]).astype(BF16).reshape(shape)

        @pl.when(d > 0)
        def _():
            db_copy(d).start()

        return carry

    def sum_a(y, carry):
        total = da_send[mx, y].astype(F32)
        for d in peers:
            total = total + da_recv[d - 1, y].astype(F32)
        ea_send[y] = total.astype(BF16)
        return carry

    def sum_b(x, carry):
        total = db_send[my, x].astype(F32)
        for d in peers:
            total = total + db_recv[d - 1, x].astype(F32)
        eb_send[x] = total.astype(BF16)
        return carry

    key_value_grads(0)
    weight_grad(0, other_rows)
    core_copy(0).start()
    weight_grad(0, own_rows)
    core_sum(0)
    z_sum(0)

    key_value_grads(1)
    lax.fori_loop(0, SIDE, latent_grads, 0)
    weight_grad(1, other_rows)
    core_copy(1).start()
    hand_over(0)
    weight_grad(1, own_rows)
    core_sum(1)
    for d in peers:
        da_copy(d).wait_recv()
    lax.fori_loop(0, SIDE, sum_a, 0)
    for d in peers:
        ea_copy(d).start()
    z_sum(1)
    for d in peers:
        db_copy(d).wait_recv()
    lax.fori_loop(0, SIDE, sum_b, 0)
    for d in peers:
        eb_copy(d).start()
    weight_out(0)
    hand_over(1)
    for d in peers:
        ea_copy(d).wait_recv()
    total = ea_send[my].astype(F32)
    for d in peers:
        total = total + ea_recv[d - 1].astype(F32)
    dlat_ref[:, :half] = total.astype(BF16)
    for d in peers:
        eb_copy(d).wait_recv()
    total = eb_send[mx].astype(F32)
    for d in peers:
        total = total + eb_recv[d - 1].astype(F32)
    dlat_ref[:, half:] = total.astype(BF16)
    weight_out(1)

    for d in peers:
        for copy in (x_first(d), y_first(d), x_second(d), y_second(d)):
            copy.wait_send()
        for copy in (da_copy(d), db_copy(d), ea_copy(d), eb_copy(d)):
            copy.wait_send()
        for head in range(heads):
            z_copy(head, d).wait_send()
            g_copy(head, d).wait_send()
    for head in range(heads):
        for i in range(2):
            out_copy(head, i).wait()
        core_copy(head).wait_send()
        for d in range(SIDE):
            h_copy(head, d).wait_send()

    def drain(n, carry):
        @pl.when(lax.rem(n, SEQ) > 0)
        def _():
            forward(n).wait_send()
            backward(n).wait_send()

        ctx_copy(n).wait()
        dq_copy(n).wait()
        return carry

    lax.fori_loop(0, heads * SEQ, drain, 0)


def whole_call(positions, slots, latents, k_weight, v_weight, queries, cotangents):
    tokens, width = queries.shape
    model, cols = k_weight.shape
    heads = cols // HD
    steps = heads * SEQ
    pair = 2 * HD
    half = model // 2
    piece = half // SIDE
    others = SIDE - 1
    smem = pl.BlockSpec(memory_space=pltpu.SMEM)
    vmem = pl.BlockSpec(memory_space=pltpu.VMEM)
    hbm = pl.BlockSpec(memory_space=pl.ANY)
    dma = pltpu.SemaphoreType.DMA
    return pl.pallas_call(
        whole_kernel,
        name="whole",
        out_shape=(
            jax.ShapeDtypeStruct((tokens, width), BF16),
            jax.ShapeDtypeStruct((tokens, width), BF16),
            jax.ShapeDtypeStruct((LATENTS, model), BF16),
            jax.ShapeDtypeStruct((model, cols), BF16),
            jax.ShapeDtypeStruct((model, cols), BF16),
        ),
        in_specs=[smem, smem, vmem, vmem, vmem, hbm, hbm],
        out_specs=(hbm, hbm, vmem, hbm, hbm),
        scratch_shapes=[
            pltpu.VMEM((SIDE, SIDE, LATENTS, model), BF16),
            pltpu.VMEM((model, SEQ * LATENTS), BF16),
            pltpu.VMEM((model, heads * pair), BF16),
            pltpu.VMEM((heads * pair, model), BF16),
            pltpu.VMEM((heads, SEQ * LATENTS, HD), F32),
            pltpu.VMEM((heads, SEQ * LATENTS, HD), F32),
            pltpu.VMEM((SEQ, LATENTS, heads * pair), BF16),
            pltpu.VMEM((steps, ROWS, pair), BF16),
            pltpu.VMEM((steps, ROWS, pair), BF16),
            pltpu.VMEM((steps, ROWS, pair), BF16),
            pltpu.VMEM((steps, ROWS, pair), BF16),
            pltpu.VMEM((SEQ * NEED, LATENTS, pair), F32),
            pltpu.VMEM((SIDE, SIDE, LATENTS, heads * pair), BF16),
            pltpu.VMEM((1, tokens), jnp.int32),
            pltpu.VMEM((steps, tokens, HD), BF16),
            pltpu.VMEM((steps, tokens, HD), BF16),
            pltpu.SMEM((SEQ,), jnp.int32),
            pltpu.SMEM((SEQ,), jnp.int32),
            pltpu.SMEM((SEQ * NEED,), jnp.int32),
            pltpu.VMEM((heads, model, pair), BF16),
            pltpu.VMEM((heads, half, pair), BF16),
            pltpu.VMEM((heads, half, pair), BF16),
            pltpu.VMEM((heads, others, piece, pair), BF16),
            pltpu.VMEM((heads, model, pair), BF16),
            pltpu.VMEM((SIDE, SIDE, LATENTS, half), BF16),
            pltpu.VMEM((SIDE, SIDE, LATENTS, half), BF16),
            pltpu.VMEM((others, SIDE, LATENTS, half), BF16),
            pltpu.VMEM((others, SIDE, LATENTS, half), BF16),
            pltpu.VMEM((SIDE, LATENTS, half), BF16),
            pltpu.VMEM((SIDE, LATENTS, half), BF16),
            pltpu.VMEM((others, LATENTS, half), BF16),
            pltpu.VMEM((others, LATENTS, half), BF16),
            dma((4, SIDE)),
            dma((4, SIDE)),
            dma((steps,)),
            dma((steps,)),
            dma((steps,)),
            dma((steps,)),
            dma((steps,)),
            dma((steps,)),
            dma((steps,)),
            dma((steps,)),
            dma((heads,)),
            dma((heads,)),
            dma((heads, SIDE)),
            dma((heads, SIDE)),
            dma((heads, SIDE)),
            dma((heads, SIDE)),
            dma((heads, SIDE)),
            dma((heads, SIDE)),
            dma((4, SIDE)),
            dma((4, SIDE)),
            dma((heads, 2)),
        ],
        compiler_params=pltpu.CompilerParams(
            collective_id=0, has_side_effects=True, vmem_limit_bytes=58 * 2**20
        ),
    )(positions, slots, latents, k_weight, v_weight, queries, cotangents)


def finish_kernel(
    ctx_in, dq_in, dk_in, dv_in, ctx_out, dq_out, dk_out, dv_out,
    ctx_buf, dq_buf, narrow, wide, in_sem, w_sem, load_sem, store_sem,
):
    parts = load_sem.shape[1]
    size = ctx_in.shape[0] // parts
    ends = ((ctx_in, ctx_buf, ctx_out), (dq_in, dq_buf, dq_out))

    def load_part(i, j):
        rows = pl.ds(i * size, size)
        src, dst, _ = ends[j]
        return pltpu.make_async_copy(src.at[rows], dst.at[rows], load_sem.at[j, i])

    def store_part(i, j):
        rows = pl.ds(i * size, size)
        _, src, dst = ends[j]
        return pltpu.make_async_copy(src.at[rows], dst.at[rows], store_sem.at[j, i])

    loads = [
        pltpu.make_async_copy(src, narrow.at[i], in_sem.at[i])
        for i, src in enumerate((dk_in, dv_in))
    ]
    stores = [
        pltpu.make_async_copy(wide.at[i], dst, w_sem.at[i]) for i, dst in enumerate((dk_out, dv_out))
    ]
    for load in loads:
        load.start()
    for i in range(parts):
        for j in range(2):
            load_part(i, j).start()
    for i in range(2):
        loads[i].wait()
        wide[i] = narrow[i].astype(F32)
        stores[i].start()
    for i in range(parts):
        for j in range(2):
            load_part(i, j).wait()
            store_part(i, j).start()
    for i in range(parts):
        for j in range(2):
            store_part(i, j).wait()
    for store in stores:
        store.wait()


def finish_call(context, d_queries, d_k, d_v):
    hbm = pl.BlockSpec(memory_space=pl.ANY)
    dma = pltpu.SemaphoreType.DMA
    return pl.pallas_call(
        finish_kernel,
        name="finish",
        out_shape=(
            jax.ShapeDtypeStruct(context.shape, BF16),
            jax.ShapeDtypeStruct(d_queries.shape, BF16),
            jax.ShapeDtypeStruct(d_k.shape, F32),
            jax.ShapeDtypeStruct(d_v.shape, F32),
        ),
        in_specs=[hbm] * 4,
        out_specs=(hbm,) * 4,
        scratch_shapes=[
            pltpu.VMEM(context.shape, BF16),
            pltpu.VMEM(context.shape, BF16),
            pltpu.VMEM((2, *d_k.shape), BF16),
            pltpu.VMEM((2, *d_k.shape), F32),
            dma((2,)),
            dma((2,)),
            dma((2, 8)),
            dma((2, 8)),
        ],
        compiler_params=pltpu.CompilerParams(vmem_limit_bytes=60 * 2**20),
    )(context, d_queries, d_k, d_v)


def local(queries, latents, k_weight, v_weight, d_context, image_pos, image_slot):
    context, d_queries, d_latents, d_k, d_v = whole_call(
        image_pos, image_slot, latents[0, 0], k_weight, v_weight, queries[0], d_context[0]
    )
    context, d_queries, d_k, d_v = finish_call(context, d_queries, d_k, d_v)
    return context[None], d_queries[None], d_latents[None, None], d_k, d_v


def solution(mesh):
    in_specs = (
        P("dp", "seq", None),
        P("dp", "seq", None, None),
        P(None, "seq"),
        P(None, "seq"),
        P("dp", "seq", None),
        P("dp", None),
        P("dp", None),
    )
    out_specs = (
        P("dp", "seq", None),
        P("dp", "seq", None),
        P("dp", "seq", None, None),
        P(None, "seq"),
        P(None, "seq"),
    )
    return jax.shard_map(local, mesh=mesh, in_specs=in_specs, out_specs=out_specs, check_vma=False)
```

```python
import math

import jax
import jax.numpy as jnp
from jax import lax
from jax.experimental import pallas as pl
from jax.experimental.pallas import tpu as pltpu
from jax.sharding import PartitionSpec as P

HD = 128
LATENTS = 64
NEED = 3
SIDE = 4
SEQ = 16
ROWS = NEED * LATENTS
EPSILON = 1e-06
SCALE = 1.0 / math.sqrt(HD)
MESH = pl.DeviceIdType.MESH
F32 = jnp.float32
BF16 = jnp.bfloat16

OFFSETS = (
    (0, 0),
    (1, 0),
    (3, 0),
    (0, 1),
    (0, 3),
    (2, 0),
    (0, 2),
    (1, 1),
    (3, 3),
    (1, 3),
    (3, 1),
    (2, 1),
    (1, 2),
    (2, 3),
    (3, 2),
    (2, 2),
)
X_CODE = sum(o[0] << (2 * i) for i, o in enumerate(OFFSETS[1:]))
Y_CODE = sum(o[1] << (2 * i) for i, o in enumerate(OFFSETS[1:]))


def offset_of(step):
    place = 2 * lax.rem(step + SEQ - 1, SEQ)
    return (
        lax.rem(lax.shift_right_logical(jnp.int32(X_CODE), place), SIDE),
        lax.rem(lax.shift_right_logical(jnp.int32(Y_CODE), place), SIDE),
    )


def nt(a, b):
    return lax.dot_general(a, b, (((1,), (1,)), ((), ())), preferred_element_type=F32)


def tn(a, b):
    return lax.dot_general(a, b, (((0,), (0,)), ((), ())), preferred_element_type=F32)


def nn(a, b):
    return lax.dot_general(a, b, (((1,), (0,)), ((), ())), preferred_element_type=F32)


def mean_last(a):
    return jnp.mean(a, axis=-1, keepdims=True)


def attend_half(query, cotangent, keys, values, image):
    raw = query.astype(F32)
    inverse = lax.rsqrt(mean_last(raw * raw) + EPSILON)
    unit = raw * inverse
    unit_b = unit.astype(BF16)
    is0, is1, is2 = image == 0, image == 1, image == 2

    def choose(wide):
        return jnp.where(
            is0, wide[:LATENTS], jnp.where(is1, wide[LATENTS : 2 * LATENTS], wide[2 * LATENTS :])
        )

    def widen(narrow):
        return jnp.concatenate(
            [jnp.where(own, narrow, 0.0).astype(BF16) for own in (is0, is1, is2)], axis=0
        )

    exponent = jnp.exp(choose(nt(keys, unit_b)) * SCALE)
    probs = exponent * (1.0 / jnp.sum(exponent, axis=0, keepdims=True))
    dprob = choose(nt(values, cotangent))
    dscore = probs * (dprob - jnp.sum(probs * dprob, axis=0, keepdims=True)) * SCALE
    probs_wide = widen(probs)
    dscore_wide = widen(dscore)
    context = tn(probs_wide, values)
    query_cot = tn(dscore_wide, keys)
    d_query = inverse * (query_cot - unit * mean_last(query_cot * unit))
    return (
        context.astype(BF16),
        d_query.astype(BF16),
        nn(dscore_wide, unit_b),
        nn(probs_wide, cotangent),
    )


def whole_kernel(
    pos_ref, slot_ref, lat_ref, kw_ref, vw_ref, q_hbm, c_hbm,
    c_buf, q_buf, dlat_ref, dk_ref, dv_ref,
    lat_all, lat_t, w_ref, w_t, unit_ref, inv_ref, kv_ref, kv_send, kv_recv, g_send, g_recv, run_ref, grad_ref, img_ref,
    first_ref, last_ref, keep_ref,
    dw_send, core_recv, z_send, z_recv, final_ref,
    da_send, db_send, da_recv, db_recv, ea_send, eb_send, ea_recv, eb_recv,
    l_ss, l_rs, f_ss, f_rs, b_ss, b_rs, q_sem, c_sem,
    core_ss, core_rs, z_ss, z_rs, g_ss, g_rs, h_ss, h_rs, d_ss, d_rs,
):
    tokens = q_hbm.shape[0]
    model = lat_ref.shape[1]
    cols = kw_ref.shape[1]
    heads = cols // HD
    pair = 2 * HD
    half = model // 2
    piece = half // SIDE
    group = SIDE * LATENTS
    peers = (1, 3, 2)
    dp = lax.axis_index("dp")
    me = lax.axis_index("seq")
    mx = lax.div(me, SIDE)
    my = lax.rem(me, SIDE)
    mz = lax.div(dp, 2)
    core = lax.rem(dp, 2)

    def ring(base, d):
        return lax.rem(base + d, SIDE)

    def peer(dx, dy):
        return (dp, ring(mx, dx) * SIDE + ring(my, dy))

    def z_peer(d):
        return (ring(mz, d) * 2 + core, me)

    core_peer = (mz * 2 + 1 - core, me)

    def owner_of(step):
        dx, dy = offset_of(step)
        return ring(mx, SIDE - dx) * SIDE + ring(my, SIDE - dy)

    def remote(src, dst, send_sem, recv_sem, device):
        return pltpu.make_async_remote_copy(
            src_ref=src,
            dst_ref=dst,
            send_sem=send_sem,
            recv_sem=recv_sem,
            device_id=device,
            device_id_type=MESH,
        )

    def lanes_of(n):
        place = owner_of(lax.rem(n, SEQ)) * cols + lax.div(n, SEQ) * HD
        return pl.ds(pl.multiple_of(place, HD), HD)

    def q_copy(n):
        return pltpu.make_async_copy(q_hbm.at[:, lanes_of(n)], q_buf.at[n], q_sem.at[n])

    def c_copy(n):
        return pltpu.make_async_copy(c_hbm.at[:, lanes_of(n)], c_buf.at[n], c_sem.at[n])

    barrier = pltpu.get_barrier_semaphore()
    for dx, dy in OFFSETS[1:]:
        pl.semaphore_signal(barrier, inc=1, device_id=peer(dx, dy), device_id_type=MESH)
    for d in peers:
        pl.semaphore_signal(barrier, inc=1, device_id=z_peer(d), device_id_type=MESH)
    pl.semaphore_signal(barrier, inc=1, device_id=core_peer, device_id_type=MESH)

    low = pl.ds(0, LATENTS // 2)
    high = pl.ds(LATENTS // 2, LATENTS // 2)

    def x_first(d):
        return remote(
            lat_ref.at[low], lat_all.at[mx, my, low], l_ss.at[0, d], l_rs.at[0, d], peer(d, 0)
        )

    def y_first(d):
        return remote(
            lat_ref.at[high], lat_all.at[mx, my, high], l_ss.at[1, d], l_rs.at[1, d], peer(0, d)
        )

    def y_second(d):
        block = lat_all.at[:, my, low]
        return remote(block, block, l_ss.at[2, d], l_rs.at[2, d], peer(0, d))

    def x_second(d):
        block = lat_all.at[mx, :, high]
        return remote(block, block, l_ss.at[3, d], l_rs.at[3, d], peer(d, 0))

    lat_all[mx, my] = lat_ref[...]
    pl.semaphore_wait(barrier, SEQ - 1 + SIDE)
    for d in peers:
        x_first(d).start()
        y_first(d).start()

    def fetch(n, carry):
        q_copy(n).start()
        c_copy(n).start()
        return carry

    lax.fori_loop(0, heads * SEQ, fetch, 0)

    for head in range(heads):
        lanes = slice(head * HD, (head + 1) * HD)
        w_ref[:, head * pair : head * pair + HD] = kw_ref[:, lanes]
        w_ref[:, head * pair + HD : (head + 1) * pair] = vw_ref[:, lanes]

    def block_images(block, carry):
        count = jnp.int32(-1)
        for i in range(SEQ):
            count = count + (pos_ref[0, i] <= block * tokens).astype(jnp.int32)
        first_ref[block] = count
        return carry

    lax.fori_loop(0, SEQ, block_images, 0)

    def slot_last(slot, carry):
        image = jnp.int32(0)
        for i in range(SEQ):
            image = image + jnp.where(slot_ref[0, i] == slot, i, 0)
        image = jnp.minimum(image, SEQ - 1)
        after = pos_ref[0, jnp.minimum(image + 1, SEQ - 1)]
        end = jnp.where(image == SEQ - 1, SEQ * tokens, after) - 1
        block = jnp.maximum(lax.div(end, tokens), 0)
        place = jnp.clip(image - first_ref[block], 0, NEED - 1)
        last_ref[slot] = block * NEED + place
        return carry

    lax.fori_loop(0, SEQ, slot_last, 0)

    token = me * tokens + lax.broadcasted_iota(jnp.int32, (1, tokens), 1)
    seen = jnp.zeros((1, tokens), jnp.int32) - 1 - first_ref[me]
    for i in range(SEQ):
        seen = seen + (token >= pos_ref[0, i]).astype(jnp.int32)
    img_ref[...] = seen

    for d in peers:
        x_first(d).wait_recv()
    for d in peers:
        y_second(d).start()
    for d in peers:
        y_first(d).wait_recv()
    for d in peers:
        x_second(d).start()
    for d in peers:
        y_second(d).wait_recv()
        x_second(d).wait_recv()

    def project(x, carry):
        rows = pl.ds(pl.multiple_of(x * group, group), group)
        slots = pl.ds(x * SIDE, SIDE)
        raw = nn(lat_all[x].reshape(group, model), w_ref[...])
        for head in range(heads):
            one = raw[:, head * pair : head * pair + HD]
            inverse = lax.rsqrt(mean_last(one * one) + EPSILON)
            unit = one * inverse
            unit_ref[head, rows, :] = unit
            inv_ref[head, rows, :] = jnp.broadcast_to(inverse, unit.shape)
            kv_ref[slots, :, head * pair : head * pair + HD] = unit.astype(BF16).reshape(
                SIDE, LATENTS, HD
            )
            values = raw[:, head * pair + HD : (head + 1) * pair].astype(BF16)
            kv_ref[slots, :, head * pair + HD : (head + 1) * pair] = values.reshape(
                SIDE, LATENTS, HD
            )
        return carry

    lax.fori_loop(0, SIDE, project, 0)

    def forward(n):
        dx, dy = offset_of(lax.rem(n, SEQ))
        return remote(kv_send.at[n], kv_recv.at[n], f_ss.at[n], f_rs.at[n], peer(dx, dy))

    def backward(n):
        place = lax.div(n, SEQ) * SEQ + me
        return remote(
            g_send.at[n],
            g_recv.at[place],
            b_ss.at[n],
            b_rs.at[place],
            (dp, owner_of(lax.rem(n, SEQ))),
        )

    def arrival(n):
        return remote(g_send.at[0], g_recv.at[n], b_ss.at[0], b_rs.at[n], (dp, lax.rem(n, SEQ)))

    def prepare(target, n, head, block):
        for j in range(NEED):
            slot = slot_ref[0, jnp.minimum(first_ref[block] + j, SEQ - 1)]
            both = kv_ref[slot]
            target[n, j * LATENTS : (j + 1) * LATENTS, :] = both[:, head * pair : (head + 1) * pair]

    for head in range(heads):

        def send(step, carry, head=head):
            n = head * SEQ + step
            dx, dy = offset_of(step)
            prepare(kv_send, n, head, peer(dx, dy)[1])
            forward(n).start()
            return carry

        lax.fori_loop(1, SEQ, send, 0)
    for head in range(heads):
        prepare(kv_recv, head * SEQ, head, me)

    def turn(x, carry):
        rows = pl.ds(pl.multiple_of(x * group, group), group)
        lat_t[:, rows] = lat_all[x].reshape(group, model).T
        return carry

    lax.fori_loop(0, SIDE, turn, 0)
    w_t[...] = w_ref[...].T

    def keep_flags(block, carry):
        first = first_ref[block]
        end = (block + 1) * tokens - 1
        before = block * tokens - 1
        last = jnp.int32(-1)
        previous = jnp.int32(-1)
        for i in range(SEQ):
            last = last + (pos_ref[0, i] <= end).astype(jnp.int32)
            previous = previous + (pos_ref[0, i] <= before).astype(jnp.int32)
        for j in range(NEED):
            same = previous == first if j == 0 else first + j > last
            keep_ref[block * NEED + j] = same.astype(jnp.int32)
        return carry

    lax.fori_loop(0, SEQ, keep_flags, 0)

    def attend(n, carry):
        own = lax.rem(n, SEQ) == 0

        @pl.when(jnp.logical_not(own))
        def _():
            forward(n).wait_recv()

        q_copy(n).wait()
        c_copy(n).wait()
        keys = kv_recv[n, :, :HD]
        values = kv_recv[n, :, HD:]
        key_part = jnp.zeros((ROWS, HD), F32)
        value_part = jnp.zeros((ROWS, HD), F32)
        size = 256
        for begin in range(0, tokens, size):
            rows = slice(begin, begin + size)
            context, d_query, key_add, value_add = attend_half(
                q_buf[n, rows, :], c_buf[n, rows, :], keys, values, img_ref[:, rows]
            )
            c_buf[n, rows, :] = context
            q_buf[n, rows, :] = d_query
            key_part = key_part + key_add
            value_part = value_part + value_add
        g_send[n, :, :HD] = key_part.astype(BF16)
        g_send[n, :, HD:] = value_part.astype(BF16)

        @pl.when(jnp.logical_not(own))
        def _():
            backward(n).start()

        @pl.when(own)
        def _():
            g_recv[lax.div(n, SEQ) * SEQ + me] = g_send[n]

        return carry

    lax.fori_loop(0, heads * SEQ, attend, 0)

    def key_value_grads(head):
        def combine(block, run):
            @pl.when(block != me)
            def _():
                arrival(head * SEQ + block).wait_recv()

            for j in range(NEED):
                keep = keep_ref[block * NEED + j].astype(F32)
                part = g_recv[head * SEQ + block, j * LATENTS : (j + 1) * LATENTS, :]
                run = run * keep + part.astype(F32)
                run_ref[block * NEED + j] = run
            return run

        lax.fori_loop(0, SEQ, combine, jnp.zeros((LATENTS, pair), F32))

        def finish(x, carry):
            rows = pl.ds(pl.multiple_of(x * group, group), group)
            total = jnp.concatenate([run_ref[last_ref[x * SIDE + y]] for y in range(SIDE)], axis=0)
            cot = total[:, :HD]
            unit = unit_ref[head, rows, :]
            key_grad = inv_ref[head, rows, :] * (cot - unit * mean_last(cot * unit))
            shape = (SIDE, LATENTS, HD)
            lanes = slice(head * pair, head * pair + HD)
            grad_ref[x, :, :, lanes] = key_grad.astype(BF16).reshape(shape)
            lanes = slice(head * pair + HD, (head + 1) * pair)
            grad_ref[x, :, :, lanes] = total[:, HD:].astype(BF16).reshape(shape)
            return carry

        lax.fori_loop(0, SIDE, finish, 0)

    own_rows = pl.multiple_of(core * half, half)
    other_rows = pl.multiple_of((1 - core) * half, half)

    def weight_grad(head, base):
        chunk = half // 2

        def one(i, carry):
            rows = pl.ds(pl.multiple_of(base + i * chunk, chunk), chunk)
            grads = grad_ref[:, :, :, head * pair : (head + 1) * pair]
            grads = grads.reshape(SEQ * LATENTS, pair)
            dw_send[head, rows, :] = nn(lat_t[rows, :], grads).astype(BF16)
            return carry

        lax.fori_loop(0, half // chunk, one, 0)

    def core_copy(head):
        return remote(
            dw_send.at[head, pl.ds(other_rows, half)],
            core_recv.at[head],
            core_ss.at[head],
            core_rs.at[head],
            core_peer,
        )

    def z_copy(head, d):
        rows = pl.ds(pl.multiple_of(ring(mz, d) * piece, piece), piece)
        return remote(
            z_send.at[head, rows],
            z_recv.at[head, d - 1],
            z_ss.at[head, d],
            z_rs.at[head, d],
            z_peer(d),
        )

    def final_rows(z, c):
        return pl.ds(pl.multiple_of(c * half + z * piece, piece), piece)

    def g_copy(head, d):
        block = final_ref.at[head, final_rows(mz, core)]
        return remote(block, block, g_ss.at[head, d], g_rs.at[head, d], z_peer(d))

    def h_copy(head, d):
        block = final_ref.at[head, final_rows(ring(mz, SIDE - d), core)]
        return remote(block, block, h_ss.at[head, d], h_rs.at[head, d], core_peer)

    def core_sum(head):
        core_copy(head).wait_recv()

        def one(i, carry):
            rows = pl.ds(pl.multiple_of(i * piece, piece), piece)
            own = pl.ds(pl.multiple_of(own_rows + i * piece, piece), piece)
            total = dw_send[head, own, :].astype(F32) + core_recv[head, rows, :].astype(F32)
            z_send[head, rows, :] = total.astype(BF16)
            return carry

        lax.fori_loop(0, SIDE, one, 0)
        for d in peers:
            z_copy(head, d).start()

    def z_sum(head):
        for d in peers:
            z_copy(head, d).wait_recv()
        total = z_send[head, pl.ds(pl.multiple_of(mz * piece, piece), piece), :].astype(F32)
        for d in peers:
            total = total + z_recv[head, d - 1].astype(F32)
        final_ref[head, final_rows(mz, core), :] = total.astype(BF16)
        for d in peers:
            g_copy(head, d).start()
        h_copy(head, 0).start()

    def hand_over(head):
        for d in peers:
            g_copy(head, d).wait_recv()
            h_copy(head, d).start()

    def weight_out(head):
        for d in range(SIDE):
            h_copy(head, d).wait_recv()
        lanes = slice(head * HD, (head + 1) * HD)

        def one(i, carry):
            rows = pl.ds(pl.multiple_of(i * piece, piece), piece)
            both = final_ref[head, rows, :].astype(F32)
            dk_ref[rows, lanes] = both[:, :HD]
            dv_ref[rows, lanes] = both[:, HD:]
            return carry

        lax.fori_loop(0, 2 * SIDE, one, 0)

    def da_copy(d):
        return remote(
            da_send.at[ring(mx, d)], da_recv.at[d - 1], d_ss.at[0, d], d_rs.at[0, d], peer(d, 0)
        )

    def db_copy(d):
        return remote(
            db_send.at[ring(my, d)], db_recv.at[d - 1], d_ss.at[1, d], d_rs.at[1, d], peer(0, d)
        )

    def ea_copy(d):
        return remote(
            ea_send.at[ring(my, d)], ea_recv.at[d - 1], d_ss.at[2, d], d_rs.at[2, d], peer(0, d)
        )

    def eb_copy(d):
        return remote(
            eb_send.at[ring(mx, d)], eb_recv.at[d - 1], d_ss.at[3, d], d_rs.at[3, d], peer(d, 0)
        )

    def latent_grads(i, carry):
        d = lax.rem(i + 1, SIDE)
        x = ring(mx, d)
        y = ring(my, d)
        shape = (SIDE, LATENTS, half)
        grads = grad_ref[x].reshape(group, heads * pair)
        da_send[x] = nn(grads, w_t[:, :half]).astype(BF16).reshape(shape)

        @pl.when(d > 0)
        def _():
            da_copy(d).start()

        grads = grad_ref[:, y].reshape(group, heads * pair)
        db_send[y] = nn(grads, w_t[:, half:]).astype(BF16).reshape(shape)

        @pl.when(d > 0)
        def _():
            db_copy(d).start()

        return carry

    def sum_a(y, carry):
        total = da_send[mx, y].astype(F32)
        for d in peers:
            total = total + da_recv[d - 1, y].astype(F32)
        ea_send[y] = total.astype(BF16)
        return carry

    def sum_b(x, carry):
        total = db_send[my, x].astype(F32)
        for d in peers:
            total = total + db_recv[d - 1, x].astype(F32)
        eb_send[x] = total.astype(BF16)
        return carry

    key_value_grads(0)
    weight_grad(0, other_rows)
    core_copy(0).start()
    weight_grad(0, own_rows)
    core_sum(0)
    z_sum(0)

    key_value_grads(1)
    lax.fori_loop(0, SIDE, latent_grads, 0)
    weight_grad(1, other_rows)
    core_copy(1).start()
    hand_over(0)
    weight_grad(1, own_rows)
    core_sum(1)
    for d in peers:
        da_copy(d).wait_recv()
    lax.fori_loop(0, SIDE, sum_a, 0)
    for d in peers:
        ea_copy(d).start()
    z_sum(1)
    for d in peers:
        db_copy(d).wait_recv()
    lax.fori_loop(0, SIDE, sum_b, 0)
    for d in peers:
        eb_copy(d).start()
    weight_out(0)
    hand_over(1)
    for d in peers:
        ea_copy(d).wait_recv()
    total = ea_send[my].astype(F32)
    for d in peers:
        total = total + ea_recv[d - 1].astype(F32)
    dlat_ref[:, :half] = total.astype(BF16)
    for d in peers:
        eb_copy(d).wait_recv()
    total = eb_send[mx].astype(F32)
    for d in peers:
        total = total + eb_recv[d - 1].astype(F32)
    dlat_ref[:, half:] = total.astype(BF16)
    weight_out(1)

    for d in peers:
        for copy in (x_first(d), y_first(d), x_second(d), y_second(d)):
            copy.wait_send()
        for copy in (da_copy(d), db_copy(d), ea_copy(d), eb_copy(d)):
            copy.wait_send()
        for head in range(heads):
            z_copy(head, d).wait_send()
            g_copy(head, d).wait_send()
    for head in range(heads):
        core_copy(head).wait_send()
        for d in range(SIDE):
            h_copy(head, d).wait_send()

    def drain(n, carry):
        @pl.when(lax.rem(n, SEQ) > 0)
        def _():
            forward(n).wait_send()
            backward(n).wait_send()

        return carry

    lax.fori_loop(0, heads * SEQ, drain, 0)


def whole_call(positions, slots, latents, k_weight, v_weight, queries, cotangents):
    tokens, width = queries.shape
    model, cols = k_weight.shape
    heads = cols // HD
    steps = heads * SEQ
    pair = 2 * HD
    half = model // 2
    piece = half // SIDE
    others = SIDE - 1
    smem = pl.BlockSpec(memory_space=pltpu.SMEM)
    vmem = pl.BlockSpec(memory_space=pltpu.VMEM)
    hbm = pl.BlockSpec(memory_space=pl.ANY)
    dma = pltpu.SemaphoreType.DMA
    return pl.pallas_call(
        whole_kernel,
        name="whole",
        out_shape=(
            pltpu.VMEM((steps, tokens, HD), BF16),
            pltpu.VMEM((steps, tokens, HD), BF16),
            pltpu.VMEM((LATENTS, model), BF16),
            pltpu.VMEM((model, cols), F32),
            pltpu.VMEM((model, cols), F32),
        ),
        in_specs=[smem, smem, vmem, vmem, vmem, hbm, hbm],
        out_specs=(vmem,) * 5,
        scratch_shapes=[
            pltpu.VMEM((SIDE, SIDE, LATENTS, model), BF16),
            pltpu.VMEM((model, SEQ * LATENTS), BF16),
            pltpu.VMEM((model, heads * pair), BF16),
            pltpu.VMEM((heads * pair, model), BF16),
            pltpu.VMEM((heads, SEQ * LATENTS, HD), F32),
            pltpu.VMEM((heads, SEQ * LATENTS, HD), F32),
            pltpu.VMEM((SEQ, LATENTS, heads * pair), BF16),
            pltpu.VMEM((steps, ROWS, pair), BF16),
            pltpu.VMEM((steps, ROWS, pair), BF16),
            pltpu.VMEM((steps, ROWS, pair), BF16),
            pltpu.VMEM((steps, ROWS, pair), BF16),
            pltpu.VMEM((SEQ * NEED, LATENTS, pair), F32),
            pltpu.VMEM((SIDE, SIDE, LATENTS, heads * pair), BF16),
            pltpu.VMEM((1, tokens), jnp.int32),
            pltpu.SMEM((SEQ,), jnp.int32),
            pltpu.SMEM((SEQ,), jnp.int32),
            pltpu.SMEM((SEQ * NEED,), jnp.int32),
            pltpu.VMEM((heads, model, pair), BF16),
            pltpu.VMEM((heads, half, pair), BF16),
            pltpu.VMEM((heads, half, pair), BF16),
            pltpu.VMEM((heads, others, piece, pair), BF16),
            pltpu.VMEM((heads, model, pair), BF16),
            pltpu.VMEM((SIDE, SIDE, LATENTS, half), BF16),
            pltpu.VMEM((SIDE, SIDE, LATENTS, half), BF16),
            pltpu.VMEM((others, SIDE, LATENTS, half), BF16),
            pltpu.VMEM((others, SIDE, LATENTS, half), BF16),
            pltpu.VMEM((SIDE, LATENTS, half), BF16),
            pltpu.VMEM((SIDE, LATENTS, half), BF16),
            pltpu.VMEM((others, LATENTS, half), BF16),
            pltpu.VMEM((others, LATENTS, half), BF16),
            dma((4, SIDE)),
            dma((4, SIDE)),
            dma((steps,)),
            dma((steps,)),
            dma((steps,)),
            dma((steps,)),
            dma((steps,)),
            dma((steps,)),
            dma((heads,)),
            dma((heads,)),
            dma((heads, SIDE)),
            dma((heads, SIDE)),
            dma((heads, SIDE)),
            dma((heads, SIDE)),
            dma((heads, SIDE)),
            dma((heads, SIDE)),
            dma((4, SIDE)),
            dma((4, SIDE)),
        ],
        compiler_params=pltpu.CompilerParams(
            collective_id=0, has_side_effects=True, vmem_limit_bytes=46 * 2**20
        ),
    )(positions, slots, latents, k_weight, v_weight, queries, cotangents)


def finish_kernel(
    ctx_in, dq_in, dk_in, dv_in, dlat_in, ctx_out, dq_out, dk_out, dv_out, dlat_out, store_sem, sem
):
    cols = dk_in.shape[1]
    me = lax.axis_index("seq")
    mx = lax.div(me, SIDE)
    my = lax.rem(me, SIDE)
    plain = [
        pltpu.make_async_copy(src, dst, sem.at[i])
        for i, (src, dst) in enumerate(((dk_in, dk_out), (dv_in, dv_out), (dlat_in, dlat_out)))
    ]

    def store(n, j):
        src, dst = ((ctx_in, ctx_out), (dq_in, dq_out))[j]
        dx, dy = offset_of(lax.rem(n, SEQ))
        owner = lax.rem(mx - dx + SIDE, SIDE) * SIDE + lax.rem(my - dy + SIDE, SIDE)
        place = owner * cols + lax.div(n, SEQ) * HD
        lanes = pl.ds(pl.multiple_of(place, HD), HD)
        return pltpu.make_async_copy(src.at[n], dst.at[:, lanes], store_sem.at[j, n])

    def start(n, carry):
        for j in range(2):
            store(n, j).start()
        return carry

    def wait(n, carry):
        for j in range(2):
            store(n, j).wait()
        return carry

    lax.fori_loop(0, ctx_in.shape[0], start, 0)
    for copy in plain:
        copy.start()
    lax.fori_loop(0, ctx_in.shape[0], wait, 0)
    for copy in plain:
        copy.wait()


def finish_call(context, d_queries, d_k, d_v, d_latents):
    hbm = pl.BlockSpec(memory_space=pl.ANY)
    dma = pltpu.SemaphoreType.DMA
    steps, tokens = context.shape[:2]
    whole = jax.ShapeDtypeStruct((tokens, steps * HD), BF16)
    return pl.pallas_call(
        finish_kernel,
        name="finish",
        out_shape=(
            whole,
            whole,
            jax.ShapeDtypeStruct(d_k.shape, F32),
            jax.ShapeDtypeStruct(d_v.shape, F32),
            jax.ShapeDtypeStruct(d_latents.shape, BF16),
        ),
        in_specs=[hbm] * 5,
        out_specs=(hbm,) * 5,
        scratch_shapes=[
            dma((2, steps)),
            dma((3,)),
        ],
        compiler_params=pltpu.CompilerParams(vmem_limit_bytes=4 * 2**20),
    )(context, d_queries, d_k, d_v, d_latents)


def local(queries, latents, k_weight, v_weight, d_context, image_pos, image_slot):
    context, d_queries, d_latents, d_k, d_v = whole_call(
        image_pos, image_slot, latents[0, 0], k_weight, v_weight, queries[0], d_context[0]
    )
    context, d_queries, d_k, d_v, d_latents = finish_call(context, d_queries, d_k, d_v, d_latents)
    return context[None], d_queries[None], d_latents[None, None], d_k, d_v


def solution(mesh):
    in_specs = (
        P("dp", "seq", None),
        P("dp", "seq", None, None),
        P(None, "seq"),
        P(None, "seq"),
        P("dp", "seq", None),
        P("dp", None),
        P("dp", None),
    )
    out_specs = (
        P("dp", "seq", None),
        P("dp", "seq", None),
        P("dp", "seq", None, None),
        P(None, "seq"),
        P(None, "seq"),
    )
    return jax.shard_map(local, mesh=mesh, in_specs=in_specs, out_specs=out_specs, check_vma=False)
```

```python
import math

import jax
import jax.numpy as jnp
from jax import lax
from jax.experimental import pallas as pl
from jax.experimental.pallas import tpu as pltpu
from jax.sharding import PartitionSpec as P

HD = 128
LATENTS = 64
NEED = 3
SIDE = 4
SEQ = 16
ROWS = NEED * LATENTS
EPSILON = 1e-06
SCALE = 1.0 / math.sqrt(HD)
MESH = pl.DeviceIdType.MESH
F32 = jnp.float32
BF16 = jnp.bfloat16

OFFSETS = (
    (0, 0),
    (1, 0),
    (3, 0),
    (0, 1),
    (0, 3),
    (2, 0),
    (0, 2),
    (1, 1),
    (3, 3),
    (1, 3),
    (3, 1),
    (2, 1),
    (1, 2),
    (2, 3),
    (3, 2),
    (2, 2),
)
X_CODE = sum(o[0] << (2 * i) for i, o in enumerate(OFFSETS[1:]))
Y_CODE = sum(o[1] << (2 * i) for i, o in enumerate(OFFSETS[1:]))


def offset_of(step):
    place = 2 * lax.rem(step + SEQ - 1, SEQ)
    return (
        lax.rem(lax.shift_right_logical(jnp.int32(X_CODE), place), SIDE),
        lax.rem(lax.shift_right_logical(jnp.int32(Y_CODE), place), SIDE),
    )


def nt(a, b):
    return lax.dot_general(a, b, (((1,), (1,)), ((), ())), preferred_element_type=F32)


def tn(a, b):
    return lax.dot_general(a, b, (((0,), (0,)), ((), ())), preferred_element_type=F32)


def nn(a, b):
    return lax.dot_general(a, b, (((1,), (0,)), ((), ())), preferred_element_type=F32)


def mean_last(a):
    return jnp.mean(a, axis=-1, keepdims=True)


def attend_half(query, cotangent, keys, values, image):
    raw = query.astype(F32)
    inverse = lax.rsqrt(mean_last(raw * raw) + EPSILON)
    unit = raw * inverse
    unit_b = unit.astype(BF16)
    is0, is1, is2 = image == 0, image == 1, image == 2

    def choose(wide):
        return jnp.where(
            is0, wide[:LATENTS], jnp.where(is1, wide[LATENTS : 2 * LATENTS], wide[2 * LATENTS :])
        )

    def widen(narrow):
        return jnp.concatenate(
            [jnp.where(own, narrow, 0.0).astype(BF16) for own in (is0, is1, is2)], axis=0
        )

    exponent = jnp.exp(choose(nt(keys, unit_b)) * SCALE)
    probs = exponent * (1.0 / jnp.sum(exponent, axis=0, keepdims=True))
    dprob = choose(nt(values, cotangent))
    dscore = probs * (dprob - jnp.sum(probs * dprob, axis=0, keepdims=True)) * SCALE
    probs_wide = widen(probs)
    dscore_wide = widen(dscore)
    context = tn(probs_wide, values)
    query_cot = tn(dscore_wide, keys)
    d_query = inverse * (query_cot - unit * mean_last(query_cot * unit))
    return (
        context.astype(BF16),
        d_query.astype(BF16),
        nn(dscore_wide, unit_b),
        nn(probs_wide, cotangent),
    )


def whole_kernel(
    pos_ref, slot_ref, lat_hbm, kw_hbm, vw_hbm, q_hbm, c_hbm,
    c_buf, q_buf, dlat_ref, dk_ref, dv_ref,
    lat_all, lat_t, w_ref, w_t, unit_ref, inv_ref, kv_ref, kv_send, kv_recv, g_send, g_recv, run_ref, grad_ref, img_ref,
    first_ref, last_ref, keep_ref,
    dw_send, core_recv, z_send, z_recv, final_ref,
    da_send, db_send, da_recv, db_recv, ea_send, eb_send, ea_recv, eb_recv,
    l_ss, l_rs, m_ss, m_rs, f_ss, f_rs, b_ss, b_rs, q_sem, in_sem,
    core_ss, core_rs, z_ss, z_rs, g_ss, g_rs, h_ss, h_rs, d_ss, d_rs,
):
    tokens = q_hbm.shape[0]
    model = lat_hbm.shape[1]
    cols = kw_hbm.shape[1]
    heads = cols // HD
    pair = 2 * HD
    half = model // 2
    piece = half // SIDE
    group = SIDE * LATENTS
    peers = (1, 3, 2)
    dp = lax.axis_index("dp")
    me = lax.axis_index("seq")
    mx = lax.div(me, SIDE)
    my = lax.rem(me, SIDE)
    mz = lax.div(dp, 2)
    core = lax.rem(dp, 2)

    def ring(base, d):
        return lax.rem(base + d, SIDE)

    def peer(dx, dy):
        return (dp, ring(mx, dx) * SIDE + ring(my, dy))

    def z_peer(d):
        return (ring(mz, d) * 2 + core, me)

    core_peer = (mz * 2 + 1 - core, me)

    def owner_of(step):
        dx, dy = offset_of(step)
        return ring(mx, SIDE - dx) * SIDE + ring(my, SIDE - dy)

    def remote(src, dst, send_sem, recv_sem, device):
        return pltpu.make_async_remote_copy(
            src_ref=src,
            dst_ref=dst,
            send_sem=send_sem,
            recv_sem=recv_sem,
            device_id=device,
            device_id_type=MESH,
        )

    def lanes_of(n):
        place = owner_of(lax.rem(n, SEQ)) * cols + lax.div(n, SEQ) * HD
        return pl.ds(pl.multiple_of(place, HD), HD)

    def fetch(i, j):
        rows = pl.ds(i * (tokens // SIDE), tokens // SIDE)
        src, dst = ((q_hbm, q_buf), (c_hbm, c_buf))[j]
        return pltpu.make_async_copy(src.at[rows], dst.at[rows], q_sem.at[i, j])

    barrier = pltpu.get_barrier_semaphore()
    for dx, dy in OFFSETS[1:]:
        pl.semaphore_signal(barrier, inc=1, device_id=peer(dx, dy), device_id_type=MESH)
    for d in peers:
        pl.semaphore_signal(barrier, inc=1, device_id=z_peer(d), device_id_type=MESH)
    pl.semaphore_signal(barrier, inc=1, device_id=core_peer, device_id_type=MESH)

    low = pl.ds(0, LATENTS // 2)
    high = pl.ds(LATENTS // 2, LATENTS // 2)

    def x_first(d):
        return remote(
            lat_hbm.at[low], lat_all.at[mx, my, low], l_ss.at[0, d], l_rs.at[0, d], peer(d, 0)
        )

    def y_first(d):
        return remote(
            lat_hbm.at[high], lat_all.at[mx, my, high], l_ss.at[1, d], l_rs.at[1, d], peer(0, d)
        )

    def y_second(s, d):
        block = lat_all.at[ring(mx, SIDE - s), my, low]
        source = lat_hbm.at[low] if s == 0 else block
        return remote(source, block, m_ss.at[0, s, d], m_rs.at[0, s, d], peer(0, d))

    def x_second(s, d):
        block = lat_all.at[mx, ring(my, SIDE - s), high]
        source = lat_hbm.at[high] if s == 0 else block
        return remote(source, block, m_ss.at[1, s, d], m_rs.at[1, s, d], peer(d, 0))

    copies = [pltpu.make_async_copy(lat_hbm, lat_all.at[mx, my], in_sem.at[0])]
    for head in range(heads):
        for i, src in enumerate((kw_hbm, vw_hbm)):
            copies.append(
                pltpu.make_async_copy(
                    src.at[:, pl.ds(head * HD, HD)],
                    w_ref.at[:, pl.ds(head * pair + i * HD, HD)],
                    in_sem.at[1 + 2 * head + i],
                )
            )
    for copy in copies:
        copy.start()
    pl.semaphore_wait(barrier, SEQ - 1 + SIDE)
    for d in peers:
        x_first(d).start()
        y_first(d).start()
    for d in peers:
        y_second(0, d).start()
        x_second(0, d).start()

    for i in range(SIDE):
        for j in range(2):
            fetch(i, j).start()

    def block_images(block, carry):
        count = jnp.int32(-1)
        for i in range(SEQ):
            count = count + (pos_ref[0, i] <= block * tokens).astype(jnp.int32)
        first_ref[block] = count
        return carry

    lax.fori_loop(0, SEQ, block_images, 0)

    def slot_last(slot, carry):
        image = jnp.int32(0)
        for i in range(SEQ):
            image = image + jnp.where(slot_ref[0, i] == slot, i, 0)
        image = jnp.minimum(image, SEQ - 1)
        after = pos_ref[0, jnp.minimum(image + 1, SEQ - 1)]
        end = jnp.where(image == SEQ - 1, SEQ * tokens, after) - 1
        block = jnp.maximum(lax.div(end, tokens), 0)
        place = jnp.clip(image - first_ref[block], 0, NEED - 1)
        last_ref[slot] = block * NEED + place
        return carry

    lax.fori_loop(0, SEQ, slot_last, 0)

    token = me * tokens + lax.broadcasted_iota(jnp.int32, (1, tokens), 1)
    seen = jnp.zeros((1, tokens), jnp.int32) - 1 - first_ref[me]
    for i in range(SEQ):
        seen = seen + (token >= pos_ref[0, i]).astype(jnp.int32)
    img_ref[...] = seen

    for s in peers:
        x_first(s).wait_recv()
        for d in peers:
            y_second(s, d).start()
        y_first(s).wait_recv()
        for d in peers:
            x_second(s, d).start()
    for s in (0, *peers):
        for d in peers:
            y_second(s, d).wait_recv()
            x_second(s, d).wait_recv()
    for copy in copies:
        copy.wait()

    def project(x, carry):
        rows = pl.ds(pl.multiple_of(x * group, group), group)
        slots = pl.ds(x * SIDE, SIDE)
        raw = nn(lat_all[x].reshape(group, model), w_ref[...])
        for head in range(heads):
            one = raw[:, head * pair : head * pair + HD]
            inverse = lax.rsqrt(mean_last(one * one) + EPSILON)
            unit = one * inverse
            unit_ref[head, rows, :] = unit
            inv_ref[head, rows, :] = jnp.broadcast_to(inverse, unit.shape)
            kv_ref[slots, :, head * pair : head * pair + HD] = unit.astype(BF16).reshape(
                SIDE, LATENTS, HD
            )
            values = raw[:, head * pair + HD : (head + 1) * pair].astype(BF16)
            kv_ref[slots, :, head * pair + HD : (head + 1) * pair] = values.reshape(
                SIDE, LATENTS, HD
            )
        return carry

    lax.fori_loop(0, SIDE, project, 0)

    def forward(n):
        dx, dy = offset_of(lax.rem(n, SEQ))
        return remote(kv_send.at[n], kv_recv.at[n], f_ss.at[n], f_rs.at[n], peer(dx, dy))

    def backward(n):
        place = lax.div(n, SEQ) * SEQ + me
        return remote(
            g_send.at[n],
            g_recv.at[place],
            b_ss.at[n],
            b_rs.at[place],
            (dp, owner_of(lax.rem(n, SEQ))),
        )

    def arrival(n):
        return remote(g_send.at[0], g_recv.at[n], b_ss.at[0], b_rs.at[n], (dp, lax.rem(n, SEQ)))

    def prepare(target, n, head, block):
        for j in range(NEED):
            slot = slot_ref[0, jnp.minimum(first_ref[block] + j, SEQ - 1)]
            both = kv_ref[slot]
            target[n, j * LATENTS : (j + 1) * LATENTS, :] = both[:, head * pair : (head + 1) * pair]

    for head in range(heads):

        def send(step, carry, head=head):
            n = head * SEQ + step
            dx, dy = offset_of(step)
            prepare(kv_send, n, head, peer(dx, dy)[1])
            forward(n).start()
            return carry

        lax.fori_loop(1, SEQ, send, 0)
    for head in range(heads):
        prepare(kv_recv, head * SEQ, head, me)

    def turn(x, carry):
        rows = pl.ds(pl.multiple_of(x * group, group), group)
        lat_t[:, rows] = lat_all[x].reshape(group, model).T
        return carry

    lax.fori_loop(0, SIDE, turn, 0)
    w_t[...] = w_ref[...].T

    def keep_flags(block, carry):
        first = first_ref[block]
        end = (block + 1) * tokens - 1
        before = block * tokens - 1
        last = jnp.int32(-1)
        previous = jnp.int32(-1)
        for i in range(SEQ):
            last = last + (pos_ref[0, i] <= end).astype(jnp.int32)
            previous = previous + (pos_ref[0, i] <= before).astype(jnp.int32)
        for j in range(NEED):
            same = previous == first if j == 0 else first + j > last
            keep_ref[block * NEED + j] = same.astype(jnp.int32)
        return carry

    lax.fori_loop(0, SEQ, keep_flags, 0)

    for i in range(SIDE):
        for j in range(2):
            fetch(i, j).wait()

    def attend(n, carry):
        own = lax.rem(n, SEQ) == 0

        @pl.when(jnp.logical_not(own))
        def _():
            forward(n).wait_recv()

        lanes = lanes_of(n)
        keys = kv_recv[n, :, :HD]
        values = kv_recv[n, :, HD:]
        key_part = jnp.zeros((ROWS, HD), F32)
        value_part = jnp.zeros((ROWS, HD), F32)
        size = 256
        for begin in range(0, tokens, size):
            rows = slice(begin, begin + size)
            context, d_query, key_add, value_add = attend_half(
                q_buf[rows, lanes], c_buf[rows, lanes], keys, values, img_ref[:, rows]
            )
            c_buf[rows, lanes] = context
            q_buf[rows, lanes] = d_query
            key_part = key_part + key_add
            value_part = value_part + value_add
        g_send[n, :, :HD] = key_part.astype(BF16)
        g_send[n, :, HD:] = value_part.astype(BF16)

        @pl.when(jnp.logical_not(own))
        def _():
            backward(n).start()

        @pl.when(own)
        def _():
            g_recv[lax.div(n, SEQ) * SEQ + me] = g_send[n]

        return carry

    lax.fori_loop(0, heads * SEQ, attend, 0)

    def key_value_grads(head):
        def combine(block, run):
            @pl.when(block != me)
            def _():
                arrival(head * SEQ + block).wait_recv()

            for j in range(NEED):
                keep = keep_ref[block * NEED + j].astype(F32)
                part = g_recv[head * SEQ + block, j * LATENTS : (j + 1) * LATENTS, :]
                run = run * keep + part.astype(F32)
                run_ref[block * NEED + j] = run
            return run

        lax.fori_loop(0, SEQ, combine, jnp.zeros((LATENTS, pair), F32))

        def finish(x, carry):
            rows = pl.ds(pl.multiple_of(x * group, group), group)
            total = jnp.concatenate([run_ref[last_ref[x * SIDE + y]] for y in range(SIDE)], axis=0)
            cot = total[:, :HD]
            unit = unit_ref[head, rows, :]
            key_grad = inv_ref[head, rows, :] * (cot - unit * mean_last(cot * unit))
            shape = (SIDE, LATENTS, HD)
            lanes = slice(head * pair, head * pair + HD)
            grad_ref[x, :, :, lanes] = key_grad.astype(BF16).reshape(shape)
            lanes = slice(head * pair + HD, (head + 1) * pair)
            grad_ref[x, :, :, lanes] = total[:, HD:].astype(BF16).reshape(shape)
            return carry

        lax.fori_loop(0, SIDE, finish, 0)

    own_rows = pl.multiple_of(core * half, half)
    other_rows = pl.multiple_of((1 - core) * half, half)

    def weight_grad(head, base):
        chunk = half // 2

        def one(i, carry):
            rows = pl.ds(pl.multiple_of(base + i * chunk, chunk), chunk)
            grads = grad_ref[:, :, :, head * pair : (head + 1) * pair]
            grads = grads.reshape(SEQ * LATENTS, pair)
            dw_send[head, rows, :] = nn(lat_t[rows, :], grads).astype(BF16)
            return carry

        lax.fori_loop(0, half // chunk, one, 0)

    def core_copy(head):
        return remote(
            dw_send.at[head, pl.ds(other_rows, half)],
            core_recv.at[head],
            core_ss.at[head],
            core_rs.at[head],
            core_peer,
        )

    def z_copy(head, d):
        rows = pl.ds(pl.multiple_of(ring(mz, d) * piece, piece), piece)
        return remote(
            z_send.at[head, rows],
            z_recv.at[head, d - 1],
            z_ss.at[head, d],
            z_rs.at[head, d],
            z_peer(d),
        )

    def final_rows(z, c):
        return pl.ds(pl.multiple_of(c * half + z * piece, piece), piece)

    def g_copy(head, d):
        block = final_ref.at[head, final_rows(mz, core)]
        return remote(block, block, g_ss.at[head, d], g_rs.at[head, d], z_peer(d))

    def h_copy(head, d):
        block = final_ref.at[head, final_rows(ring(mz, SIDE - d), core)]
        return remote(block, block, h_ss.at[head, d], h_rs.at[head, d], core_peer)

    def core_sum(head):
        core_copy(head).wait_recv()

        def one(i, carry):
            rows = pl.ds(pl.multiple_of(i * piece, piece), piece)
            own = pl.ds(pl.multiple_of(own_rows + i * piece, piece), piece)
            total = dw_send[head, own, :].astype(F32) + core_recv[head, rows, :].astype(F32)
            z_send[head, rows, :] = total.astype(BF16)
            return carry

        lax.fori_loop(0, SIDE, one, 0)
        for d in peers:
            z_copy(head, d).start()

    def z_sum(head):
        for d in peers:
            z_copy(head, d).wait_recv()
        total = z_send[head, pl.ds(pl.multiple_of(mz * piece, piece), piece), :].astype(F32)
        for d in peers:
            total = total + z_recv[head, d - 1].astype(F32)
        final_ref[head, final_rows(mz, core), :] = total.astype(BF16)
        for d in peers:
            g_copy(head, d).start()
        h_copy(head, 0).start()

    def hand_over(head):
        for d in peers:
            g_copy(head, d).wait_recv()
            h_copy(head, d).start()

    def weight_out(head):
        for d in range(SIDE):
            h_copy(head, d).wait_recv()
        lanes = slice(head * HD, (head + 1) * HD)

        def one(i, carry):
            rows = pl.ds(pl.multiple_of(i * piece, piece), piece)
            both = final_ref[head, rows, :].astype(F32)
            dk_ref[rows, lanes] = both[:, :HD]
            dv_ref[rows, lanes] = both[:, HD:]
            return carry

        lax.fori_loop(0, 2 * SIDE, one, 0)

    def da_copy(d, e):
        y = ring(my, e)
        return remote(
            da_send.at[ring(mx, d), y],
            da_recv.at[d - 1, y],
            d_ss.at[0, d, e],
            d_rs.at[0, d, e],
            peer(d, 0),
        )

    def db_copy(d, e):
        x = ring(mx, e)
        return remote(
            db_send.at[ring(my, d), x],
            db_recv.at[d - 1, x],
            d_ss.at[1, d, e],
            d_rs.at[1, d, e],
            peer(0, d),
        )

    def ea_copy(d):
        return remote(
            ea_send.at[ring(my, d)], ea_recv.at[d - 1], d_ss.at[2, 0, d], d_rs.at[2, 0, d], peer(0, d)
        )

    def eb_copy(d):
        return remote(
            eb_send.at[ring(mx, d)], eb_recv.at[d - 1], d_ss.at[3, 0, d], d_rs.at[3, 0, d], peer(d, 0)
        )

    order = (*peers, 0)

    def latent_grads(i, carry):
        d = lax.rem(i + 1, SIDE)
        x = ring(mx, d)
        y = ring(my, d)
        shape = (SIDE, LATENTS, half)
        grads = grad_ref[x].reshape(group, heads * pair)
        da_send[x] = nn(grads, w_t[:, :half]).astype(BF16).reshape(shape)

        @pl.when(d > 0)
        def _():
            for e in order[:2]:
                da_copy(d, e).start()

        grads = grad_ref[:, y].reshape(group, heads * pair)
        db_send[y] = nn(grads, w_t[:, half:]).astype(BF16).reshape(shape)

        @pl.when(d > 0)
        def _():
            for e in order[:2]:
                db_copy(d, e).start()

        return carry

    def latent_send(e):
        for d in peers:
            da_copy(d, e).start()
            db_copy(d, e).start()

    def latent_step(e):
        y = ring(my, e)
        x = ring(mx, e)
        for d in peers:
            da_copy(d, e).wait_recv()
        total = da_send[mx, y].astype(F32)
        for d in peers:
            total = total + da_recv[d - 1, y].astype(F32)
        ea_send[y] = total.astype(BF16)
        if e:
            ea_copy(e).start()
        for d in peers:
            db_copy(d, e).wait_recv()
        total = db_send[my, x].astype(F32)
        for d in peers:
            total = total + db_recv[d - 1, x].astype(F32)
        eb_send[x] = total.astype(BF16)
        if e:
            eb_copy(e).start()

    key_value_grads(0)
    weight_grad(0, other_rows)
    core_copy(0).start()
    weight_grad(0, own_rows)
    core_sum(0)
    z_sum(0)

    key_value_grads(1)
    weight_grad(1, other_rows)
    core_copy(1).start()
    lax.fori_loop(0, SIDE, latent_grads, 0)
    weight_grad(1, own_rows)
    core_sum(1)
    hand_over(0)
    latent_step(1)
    latent_send(2)
    z_sum(1)
    latent_step(3)
    latent_send(0)
    weight_out(0)
    latent_step(2)
    hand_over(1)
    latent_step(0)
    for d in peers:
        ea_copy(d).wait_recv()
    total = ea_send[my].astype(F32)
    for d in peers:
        total = total + ea_recv[d - 1].astype(F32)
    dlat_ref[:, :half] = total.astype(BF16)
    for d in peers:
        eb_copy(d).wait_recv()
    total = eb_send[mx].astype(F32)
    for d in peers:
        total = total + eb_recv[d - 1].astype(F32)
    dlat_ref[:, half:] = total.astype(BF16)
    weight_out(1)

    for d in peers:
        x_first(d).wait_send()
        y_first(d).wait_send()
        ea_copy(d).wait_send()
        eb_copy(d).wait_send()
        for s in (0, *peers):
            x_second(s, d).wait_send()
            y_second(s, d).wait_send()
            da_copy(d, s).wait_send()
            db_copy(d, s).wait_send()
        for head in range(heads):
            z_copy(head, d).wait_send()
            g_copy(head, d).wait_send()
    for head in range(heads):
        core_copy(head).wait_send()
        for d in range(SIDE):
            h_copy(head, d).wait_send()

    def drain(n, carry):
        @pl.when(lax.rem(n, SEQ) > 0)
        def _():
            forward(n).wait_send()
            backward(n).wait_send()

        return carry

    lax.fori_loop(0, heads * SEQ, drain, 0)


def whole_call(positions, slots, latents, k_weight, v_weight, queries, cotangents):
    tokens, width = queries.shape
    model, cols = k_weight.shape
    heads = cols // HD
    steps = heads * SEQ
    pair = 2 * HD
    half = model // 2
    piece = half // SIDE
    others = SIDE - 1
    smem = pl.BlockSpec(memory_space=pltpu.SMEM)
    vmem = pl.BlockSpec(memory_space=pltpu.VMEM)
    hbm = pl.BlockSpec(memory_space=pl.ANY)
    dma = pltpu.SemaphoreType.DMA
    return pl.pallas_call(
        whole_kernel,
        name="whole",
        out_shape=(
            pltpu.VMEM((tokens, width), BF16),
            pltpu.VMEM((tokens, width), BF16),
            pltpu.VMEM((LATENTS, model), BF16),
            pltpu.VMEM((model, cols), F32),
            pltpu.VMEM((model, cols), F32),
        ),
        in_specs=[smem, smem, hbm, hbm, hbm, hbm, hbm],
        out_specs=(vmem,) * 5,
        scratch_shapes=[
            pltpu.VMEM((SIDE, SIDE, LATENTS, model), BF16),
            pltpu.VMEM((model, SEQ * LATENTS), BF16),
            pltpu.VMEM((model, heads * pair), BF16),
            pltpu.VMEM((heads * pair, model), BF16),
            pltpu.VMEM((heads, SEQ * LATENTS, HD), F32),
            pltpu.VMEM((heads, SEQ * LATENTS, HD), F32),
            pltpu.VMEM((SEQ, LATENTS, heads * pair), BF16),
            pltpu.VMEM((steps, ROWS, pair), BF16),
            pltpu.VMEM((steps, ROWS, pair), BF16),
            pltpu.VMEM((steps, ROWS, pair), BF16),
            pltpu.VMEM((steps, ROWS, pair), BF16),
            pltpu.VMEM((SEQ * NEED, LATENTS, pair), F32),
            pltpu.VMEM((SIDE, SIDE, LATENTS, heads * pair), BF16),
            pltpu.VMEM((1, tokens), jnp.int32),
            pltpu.SMEM((SEQ,), jnp.int32),
            pltpu.SMEM((SEQ,), jnp.int32),
            pltpu.SMEM((SEQ * NEED,), jnp.int32),
            pltpu.VMEM((heads, model, pair), BF16),
            pltpu.VMEM((heads, half, pair), BF16),
            pltpu.VMEM((heads, half, pair), BF16),
            pltpu.VMEM((heads, others, piece, pair), BF16),
            pltpu.VMEM((heads, model, pair), BF16),
            pltpu.VMEM((SIDE, SIDE, LATENTS, half), BF16),
            pltpu.VMEM((SIDE, SIDE, LATENTS, half), BF16),
            pltpu.VMEM((others, SIDE, LATENTS, half), BF16),
            pltpu.VMEM((others, SIDE, LATENTS, half), BF16),
            pltpu.VMEM((SIDE, LATENTS, half), BF16),
            pltpu.VMEM((SIDE, LATENTS, half), BF16),
            pltpu.VMEM((others, LATENTS, half), BF16),
            pltpu.VMEM((others, LATENTS, half), BF16),
            dma((2, SIDE)),
            dma((2, SIDE)),
            dma((2, SIDE, SIDE)),
            dma((2, SIDE, SIDE)),
            dma((steps,)),
            dma((steps,)),
            dma((steps,)),
            dma((steps,)),
            dma((SIDE, 2)),
            dma((1 + 2 * heads,)),
            dma((heads,)),
            dma((heads,)),
            dma((heads, SIDE)),
            dma((heads, SIDE)),
            dma((heads, SIDE)),
            dma((heads, SIDE)),
            dma((heads, SIDE)),
            dma((heads, SIDE)),
            dma((4, SIDE, SIDE)),
            dma((4, SIDE, SIDE)),
        ],
        compiler_params=pltpu.CompilerParams(
            collective_id=0, has_side_effects=True, vmem_limit_bytes=46 * 2**20
        ),
    )(positions, slots, latents, k_weight, v_weight, queries, cotangents)


def finish_kernel(
    ctx_in, dq_in, dk_in, dv_in, dlat_in, ctx_out, dq_out, dk_out, dv_out, dlat_out, sems, lat_sem
):
    copies = [pltpu.make_async_copy(dlat_in, dlat_out, lat_sem)]
    parts = sems.shape[1]
    pairs = ((ctx_in, ctx_out), (dq_in, dq_out), (dk_in, dk_out), (dv_in, dv_out))
    for j, (src, dst) in enumerate(pairs):
        size = src.shape[0] // parts
        for i in range(parts):
            rows = pl.ds(i * size, size)
            copies.append(pltpu.make_async_copy(src.at[rows], dst.at[rows], sems.at[j, i]))
    for copy in copies:
        copy.start()
    for copy in copies:
        copy.wait()


def finish_call(context, d_queries, d_k, d_v, d_latents):
    hbm = pl.BlockSpec(memory_space=pl.ANY)
    dma = pltpu.SemaphoreType.DMA
    whole = jax.ShapeDtypeStruct(context.shape, BF16)
    return pl.pallas_call(
        finish_kernel,
        name="finish",
        out_shape=(
            whole,
            whole,
            jax.ShapeDtypeStruct(d_k.shape, F32),
            jax.ShapeDtypeStruct(d_v.shape, F32),
            jax.ShapeDtypeStruct(d_latents.shape, BF16),
        ),
        in_specs=[hbm] * 5,
        out_specs=(hbm,) * 5,
        scratch_shapes=[
            dma((4, 4)),
            dma(()),
        ],
        compiler_params=pltpu.CompilerParams(vmem_limit_bytes=4 * 2**20),
    )(context, d_queries, d_k, d_v, d_latents)


def local(queries, latents, k_weight, v_weight, d_context, image_pos, image_slot):
    context, d_queries, d_latents, d_k, d_v = whole_call(
        image_pos, image_slot, latents[0, 0], k_weight, v_weight, queries[0], d_context[0]
    )
    context, d_queries, d_k, d_v, d_latents = finish_call(context, d_queries, d_k, d_v, d_latents)
    return context[None], d_queries[None], d_latents[None, None], d_k, d_v


def solution(mesh):
    in_specs = (
        P("dp", "seq", None),
        P("dp", "seq", None, None),
        P(None, "seq"),
        P(None, "seq"),
        P("dp", "seq", None),
        P("dp", None),
        P("dp", None),
    )
    out_specs = (
        P("dp", "seq", None),
        P("dp", "seq", None),
        P("dp", "seq", None, None),
        P(None, "seq"),
        P(None, "seq"),
    )
    return jax.shard_map(local, mesh=mesh, in_specs=in_specs, out_specs=out_specs, check_vma=False)
```

```python
import math

import jax
import jax.numpy as jnp
from jax import lax
from jax.experimental import pallas as pl
from jax.experimental.pallas import tpu as pltpu
from jax.sharding import PartitionSpec as P

HD = 128
LATENTS = 64
NEED = 3
SIDE = 4
SEQ = 16
ROWS = NEED * LATENTS
EPSILON = 1e-06
SCALE = 1.0 / math.sqrt(HD)
MESH = pl.DeviceIdType.MESH
F32 = jnp.float32
BF16 = jnp.bfloat16

OFFSETS = (
    (0, 0),
    (1, 0),
    (3, 0),
    (0, 1),
    (0, 3),
    (2, 0),
    (0, 2),
    (1, 1),
    (3, 3),
    (1, 3),
    (3, 1),
    (2, 1),
    (1, 2),
    (2, 3),
    (3, 2),
    (2, 2),
)
X_CODE = sum(o[0] << (2 * i) for i, o in enumerate(OFFSETS[1:]))
Y_CODE = sum(o[1] << (2 * i) for i, o in enumerate(OFFSETS[1:]))


def offset_of(step):
    place = 2 * lax.rem(step + SEQ - 1, SEQ)
    return (
        lax.rem(lax.shift_right_logical(jnp.int32(X_CODE), place), SIDE),
        lax.rem(lax.shift_right_logical(jnp.int32(Y_CODE), place), SIDE),
    )


def nt(a, b):
    return lax.dot_general(a, b, (((1,), (1,)), ((), ())), preferred_element_type=F32)


def tn(a, b):
    return lax.dot_general(a, b, (((0,), (0,)), ((), ())), preferred_element_type=F32)


def nn(a, b):
    return lax.dot_general(a, b, (((1,), (0,)), ((), ())), preferred_element_type=F32)


def mean_last(a):
    return jnp.mean(a, axis=-1, keepdims=True)


def attend_half(query, cotangent, keys, values, image):
    raw = query.astype(F32)
    inverse = lax.rsqrt(mean_last(raw * raw) + EPSILON)
    unit = raw * inverse
    unit_b = unit.astype(BF16)
    is0, is1, is2 = image == 0, image == 1, image == 2

    def choose(wide):
        return jnp.where(
            is0, wide[:LATENTS], jnp.where(is1, wide[LATENTS : 2 * LATENTS], wide[2 * LATENTS :])
        )

    def widen(narrow):
        return jnp.concatenate(
            [jnp.where(own, narrow, 0.0).astype(BF16) for own in (is0, is1, is2)], axis=0
        )

    exponent = jnp.exp(choose(nt(keys, unit_b)) * SCALE)
    probs = exponent * (1.0 / jnp.sum(exponent, axis=0, keepdims=True))
    dprob = choose(nt(values, cotangent))
    dscore = probs * (dprob - jnp.sum(probs * dprob, axis=0, keepdims=True)) * SCALE
    probs_wide = widen(probs)
    dscore_wide = widen(dscore)
    context = tn(probs_wide, values)
    query_cot = tn(dscore_wide, keys)
    d_query = inverse * (query_cot - unit * mean_last(query_cot * unit))
    return (
        context.astype(BF16),
        d_query.astype(BF16),
        nn(dscore_wide, unit_b),
        nn(probs_wide, cotangent),
    )


def whole_kernel(
    pos_ref, slot_ref, lat_hbm, kw_hbm, vw_hbm, q_hbm, c_hbm,
    c_buf, q_buf, dlat_ref, dk_ref, dv_ref,
    lat_all, lat_t, w_ref, w_t, unit_ref, inv_ref, kv_ref, kv_send, kv_recv, g_send, g_recv, run_ref, grad_ref, img_ref,
    first_ref, last_ref, keep_ref,
    dw_send, core_recv, z_send, z_recv, final_ref,
    da_send, db_send, da_recv, db_recv, ea_send, eb_send, ea_recv, eb_recv,
    l_ss, l_rs, m_ss, m_rs, f_ss, f_rs, b_ss, b_rs, q_sem, in_sem,
    core_ss, core_rs, z_ss, z_rs, g_ss, g_rs, h_ss, h_rs, d_ss, d_rs,
):
    tokens = q_hbm.shape[0]
    model = lat_hbm.shape[1]
    cols = kw_hbm.shape[1]
    heads = cols // HD
    pair = 2 * HD
    half = model // 2
    piece = half // SIDE
    group = SIDE * LATENTS
    peers = (1, 3, 2)
    dp = lax.axis_index("dp")
    me = lax.axis_index("seq")
    mx = lax.div(me, SIDE)
    my = lax.rem(me, SIDE)
    mz = lax.div(dp, 2)
    core = lax.rem(dp, 2)

    def ring(base, d):
        return lax.rem(base + d, SIDE)

    def peer(dx, dy):
        return (dp, ring(mx, dx) * SIDE + ring(my, dy))

    def z_peer(d):
        return (ring(mz, d) * 2 + core, me)

    core_peer = (mz * 2 + 1 - core, me)

    def owner_of(step):
        dx, dy = offset_of(step)
        return ring(mx, SIDE - dx) * SIDE + ring(my, SIDE - dy)

    def remote(src, dst, send_sem, recv_sem, device):
        return pltpu.make_async_remote_copy(
            src_ref=src,
            dst_ref=dst,
            send_sem=send_sem,
            recv_sem=recv_sem,
            device_id=device,
            device_id_type=MESH,
        )

    def lanes_of(n):
        place = owner_of(lax.rem(n, SEQ)) * cols + lax.div(n, SEQ) * HD
        return pl.ds(pl.multiple_of(place, HD), HD)

    def fetch(i, j):
        rows = pl.ds(i * (tokens // SIDE), tokens // SIDE)
        src, dst = ((q_hbm, q_buf), (c_hbm, c_buf))[j]
        return pltpu.make_async_copy(src.at[rows], dst.at[rows], q_sem.at[i, j])

    barrier = pltpu.get_barrier_semaphore()
    for dx, dy in OFFSETS[1:]:
        pl.semaphore_signal(barrier, inc=1, device_id=peer(dx, dy), device_id_type=MESH)
    for d in peers:
        pl.semaphore_signal(barrier, inc=1, device_id=z_peer(d), device_id_type=MESH)
    pl.semaphore_signal(barrier, inc=1, device_id=core_peer, device_id_type=MESH)

    low = pl.ds(0, LATENTS // 2)
    high = pl.ds(LATENTS // 2, LATENTS // 2)

    def x_first(d):
        return remote(
            lat_hbm.at[low], lat_all.at[mx, my, low], l_ss.at[0, d], l_rs.at[0, d], peer(d, 0)
        )

    def y_first(d):
        return remote(
            lat_hbm.at[high], lat_all.at[mx, my, high], l_ss.at[1, d], l_rs.at[1, d], peer(0, d)
        )

    part_rows = LATENTS // 4
    hops = ((0, 1, 0, 2), (0, 3, 0, 2), (1, 1, 0, 1), (3, 3, 1, 1))

    def second(kind, s, hop):
        back, d, begin, parts = hops[hop]
        rows = pl.ds((2 * kind + begin) * part_rows, parts * part_rows)
        x, y = ((s, back), (back, s))[kind]
        block = lat_all.at[ring(mx, SIDE - x), ring(my, SIDE - y), rows]
        source = lat_hbm.at[rows] if back == 0 and s == 0 else block
        target = peer(d, 0) if kind else peer(0, d)
        return remote(source, block, m_ss.at[kind, s, hop], m_rs.at[kind, s, hop], target)

    def spread(s):
        for hop in (0, 1):
            for kind in range(2):
                second(kind, s, hop).start()

    def pass_on(s):
        for hop in (0, 1):
            for kind in range(2):
                second(kind, s, hop).wait_recv()
                second(kind, s, hop + 2).start()

    copies = [pltpu.make_async_copy(lat_hbm, lat_all.at[mx, my], in_sem.at[0])]
    for head in range(heads):
        for i, src in enumerate((kw_hbm, vw_hbm)):
            copies.append(
                pltpu.make_async_copy(
                    src.at[:, pl.ds(head * HD, HD)],
                    w_ref.at[:, pl.ds(head * pair + i * HD, HD)],
                    in_sem.at[1 + 2 * head + i],
                )
            )
    for copy in copies:
        copy.start()
    pl.semaphore_wait(barrier, SEQ - 1 + SIDE)
    for d in peers:
        x_first(d).start()
        y_first(d).start()
    spread(0)

    for i in range(SIDE):
        for j in range(2):
            fetch(i, j).start()

    def block_images(block, carry):
        count = jnp.int32(-1)
        for i in range(SEQ):
            count = count + (pos_ref[0, i] <= block * tokens).astype(jnp.int32)
        first_ref[block] = count
        return carry

    lax.fori_loop(0, SEQ, block_images, 0)

    def slot_last(slot, carry):
        image = jnp.int32(0)
        for i in range(SEQ):
            image = image + jnp.where(slot_ref[0, i] == slot, i, 0)
        image = jnp.minimum(image, SEQ - 1)
        after = pos_ref[0, jnp.minimum(image + 1, SEQ - 1)]
        end = jnp.where(image == SEQ - 1, SEQ * tokens, after) - 1
        block = jnp.maximum(lax.div(end, tokens), 0)
        place = jnp.clip(image - first_ref[block], 0, NEED - 1)
        last_ref[slot] = block * NEED + place
        return carry

    lax.fori_loop(0, SEQ, slot_last, 0)

    token = me * tokens + lax.broadcasted_iota(jnp.int32, (1, tokens), 1)
    seen = jnp.zeros((1, tokens), jnp.int32) - 1 - first_ref[me]
    for i in range(SEQ):
        seen = seen + (token >= pos_ref[0, i]).astype(jnp.int32)
    img_ref[...] = seen

    for s, settled in ((1, 0), (3, 1), (2, 3)):
        x_first(s).wait_recv()
        y_first(s).wait_recv()
        spread(s)
        pass_on(settled)
    pass_on(2)
    for s in range(SIDE):
        for kind in range(2):
            second(kind, s, 2).wait_recv()
            second(kind, s, 3).wait_recv()
    for copy in copies:
        copy.wait()

    def project(x, carry):
        rows = pl.ds(pl.multiple_of(x * group, group), group)
        slots = pl.ds(x * SIDE, SIDE)
        raw = nn(lat_all[x].reshape(group, model), w_ref[...])
        for head in range(heads):
            one = raw[:, head * pair : head * pair + HD]
            inverse = lax.rsqrt(mean_last(one * one) + EPSILON)
            unit = one * inverse
            unit_ref[head, rows, :] = unit
            inv_ref[head, rows, :] = jnp.broadcast_to(inverse, unit.shape)
            kv_ref[slots, :, head * pair : head * pair + HD] = unit.astype(BF16).reshape(
                SIDE, LATENTS, HD
            )
            values = raw[:, head * pair + HD : (head + 1) * pair].astype(BF16)
            kv_ref[slots, :, head * pair + HD : (head + 1) * pair] = values.reshape(
                SIDE, LATENTS, HD
            )
        return carry

    lax.fori_loop(0, SIDE, project, 0)

    def forward(n):
        dx, dy = offset_of(lax.rem(n, SEQ))
        return remote(kv_send.at[n], kv_recv.at[n], f_ss.at[n], f_rs.at[n], peer(dx, dy))

    def backward(n):
        place = lax.div(n, SEQ) * SEQ + me
        return remote(
            g_send.at[n],
            g_recv.at[place],
            b_ss.at[n],
            b_rs.at[place],
            (dp, owner_of(lax.rem(n, SEQ))),
        )

    def arrival(n):
        return remote(g_send.at[0], g_recv.at[n], b_ss.at[0], b_rs.at[n], (dp, lax.rem(n, SEQ)))

    def prepare(target, n, head, block):
        for j in range(NEED):
            slot = slot_ref[0, jnp.minimum(first_ref[block] + j, SEQ - 1)]
            both = kv_ref[slot]
            target[n, j * LATENTS : (j + 1) * LATENTS, :] = both[:, head * pair : (head + 1) * pair]

    for head in range(heads):

        def send(step, carry, head=head):
            n = head * SEQ + step
            dx, dy = offset_of(step)
            prepare(kv_send, n, head, peer(dx, dy)[1])
            forward(n).start()
            return carry

        lax.fori_loop(1, SEQ, send, 0)
    for head in range(heads):
        prepare(kv_recv, head * SEQ, head, me)

    def turn(x, carry):
        rows = pl.ds(pl.multiple_of(x * group, group), group)
        lat_t[:, rows] = lat_all[x].reshape(group, model).T
        return carry

    lax.fori_loop(0, SIDE, turn, 0)
    w_t[...] = w_ref[...].T

    def keep_flags(block, carry):
        first = first_ref[block]
        end = (block + 1) * tokens - 1
        before = block * tokens - 1
        last = jnp.int32(-1)
        previous = jnp.int32(-1)
        for i in range(SEQ):
            last = last + (pos_ref[0, i] <= end).astype(jnp.int32)
            previous = previous + (pos_ref[0, i] <= before).astype(jnp.int32)
        for j in range(NEED):
            same = previous == first if j == 0 else first + j > last
            keep_ref[block * NEED + j] = same.astype(jnp.int32)
        return carry

    lax.fori_loop(0, SEQ, keep_flags, 0)

    for i in range(SIDE):
        for j in range(2):
            fetch(i, j).wait()

    def attend(n, carry):
        own = lax.rem(n, SEQ) == 0

        @pl.when(jnp.logical_not(own))
        def _():
            forward(n).wait_recv()

        lanes = lanes_of(n)
        keys = kv_recv[n, :, :HD]
        values = kv_recv[n, :, HD:]
        key_part = jnp.zeros((ROWS, HD), F32)
        value_part = jnp.zeros((ROWS, HD), F32)
        size = 256
        for begin in range(0, tokens, size):
            rows = slice(begin, begin + size)
            context, d_query, key_add, value_add = attend_half(
                q_buf[rows, lanes], c_buf[rows, lanes], keys, values, img_ref[:, rows]
            )
            c_buf[rows, lanes] = context
            q_buf[rows, lanes] = d_query
            key_part = key_part + key_add
            value_part = value_part + value_add
        g_send[n, :, :HD] = key_part.astype(BF16)
        g_send[n, :, HD:] = value_part.astype(BF16)

        @pl.when(jnp.logical_not(own))
        def _():
            backward(n).start()

        @pl.when(own)
        def _():
            g_recv[lax.div(n, SEQ) * SEQ + me] = g_send[n]

        return carry

    lax.fori_loop(0, heads * SEQ, attend, 0)

    def key_value_grads(head):
        def combine(block, run):
            @pl.when(block != me)
            def _():
                arrival(head * SEQ + block).wait_recv()

            for j in range(NEED):
                keep = keep_ref[block * NEED + j].astype(F32)
                part = g_recv[head * SEQ + block, j * LATENTS : (j + 1) * LATENTS, :]
                run = run * keep + part.astype(F32)
                run_ref[block * NEED + j] = run
            return run

        lax.fori_loop(0, SEQ, combine, jnp.zeros((LATENTS, pair), F32))

        def finish(x, carry):
            rows = pl.ds(pl.multiple_of(x * group, group), group)
            total = jnp.concatenate([run_ref[last_ref[x * SIDE + y]] for y in range(SIDE)], axis=0)
            cot = total[:, :HD]
            unit = unit_ref[head, rows, :]
            key_grad = inv_ref[head, rows, :] * (cot - unit * mean_last(cot * unit))
            shape = (SIDE, LATENTS, HD)
            lanes = slice(head * pair, head * pair + HD)
            grad_ref[x, :, :, lanes] = key_grad.astype(BF16).reshape(shape)
            lanes = slice(head * pair + HD, (head + 1) * pair)
            grad_ref[x, :, :, lanes] = total[:, HD:].astype(BF16).reshape(shape)
            return carry

        lax.fori_loop(0, SIDE, finish, 0)

    own_rows = pl.multiple_of(core * half, half)
    other_rows = pl.multiple_of((1 - core) * half, half)

    def weight_grad(head, base):
        chunk = half // 2

        def one(i, carry):
            rows = pl.ds(pl.multiple_of(base + i * chunk, chunk), chunk)
            grads = grad_ref[:, :, :, head * pair : (head + 1) * pair]
            grads = grads.reshape(SEQ * LATENTS, pair)
            dw_send[head, rows, :] = nn(lat_t[rows, :], grads).astype(BF16)
            return carry

        lax.fori_loop(0, half // chunk, one, 0)

    def core_copy(head):
        return remote(
            dw_send.at[head, pl.ds(other_rows, half)],
            core_recv.at[head],
            core_ss.at[head],
            core_rs.at[head],
            core_peer,
        )

    def z_copy(head, d):
        rows = pl.ds(pl.multiple_of(ring(mz, d) * piece, piece), piece)
        return remote(
            z_send.at[head, rows],
            z_recv.at[head, d - 1],
            z_ss.at[head, d],
            z_rs.at[head, d],
            z_peer(d),
        )

    def final_rows(z, c):
        return pl.ds(pl.multiple_of(c * half + z * piece, piece), piece)

    def g_copy(head, d):
        block = final_ref.at[head, final_rows(mz, core)]
        return remote(block, block, g_ss.at[head, d], g_rs.at[head, d], z_peer(d))

    def h_copy(head, d):
        block = final_ref.at[head, final_rows(ring(mz, SIDE - d), core)]
        return remote(block, block, h_ss.at[head, d], h_rs.at[head, d], core_peer)

    def core_sum(head):
        core_copy(head).wait_recv()

        def one(i, carry):
            rows = pl.ds(pl.multiple_of(i * piece, piece), piece)
            own = pl.ds(pl.multiple_of(own_rows + i * piece, piece), piece)
            total = dw_send[head, own, :].astype(F32) + core_recv[head, rows, :].astype(F32)
            z_send[head, rows, :] = total.astype(BF16)
            return carry

        lax.fori_loop(0, SIDE, one, 0)
        for d in peers:
            z_copy(head, d).start()

    def z_sum(head):
        for d in peers:
            z_copy(head, d).wait_recv()
        total = z_send[head, pl.ds(pl.multiple_of(mz * piece, piece), piece), :].astype(F32)
        for d in peers:
            total = total + z_recv[head, d - 1].astype(F32)
        final_ref[head, final_rows(mz, core), :] = total.astype(BF16)
        for d in peers:
            g_copy(head, d).start()
        h_copy(head, 0).start()

    def hand_over(head):
        for d in peers:
            g_copy(head, d).wait_recv()
            h_copy(head, d).start()

    def weight_out(head):
        for d in range(SIDE):
            h_copy(head, d).wait_recv()
        lanes = slice(head * HD, (head + 1) * HD)

        def one(i, carry):
            rows = pl.ds(pl.multiple_of(i * piece, piece), piece)
            both = final_ref[head, rows, :].astype(F32)
            dk_ref[rows, lanes] = both[:, :HD]
            dv_ref[rows, lanes] = both[:, HD:]
            return carry

        lax.fori_loop(0, 2 * SIDE, one, 0)

    def da_copy(d, e):
        y = ring(my, e)
        return remote(
            da_send.at[ring(mx, d), y],
            da_recv.at[d - 1, y],
            d_ss.at[0, d, e],
            d_rs.at[0, d, e],
            peer(d, 0),
        )

    def db_copy(d, e):
        x = ring(mx, e)
        return remote(
            db_send.at[ring(my, d), x],
            db_recv.at[d - 1, x],
            d_ss.at[1, d, e],
            d_rs.at[1, d, e],
            peer(0, d),
        )

    def ea_copy(d):
        return remote(
            ea_send.at[ring(my, d)], ea_recv.at[d - 1], d_ss.at[2, 0, d], d_rs.at[2, 0, d], peer(0, d)
        )

    def eb_copy(d):
        return remote(
            eb_send.at[ring(mx, d)], eb_recv.at[d - 1], d_ss.at[3, 0, d], d_rs.at[3, 0, d], peer(d, 0)
        )

    order = (*peers, 0)

    def latent_grads(i, carry):
        d = lax.rem(i + 1, SIDE)
        x = ring(mx, d)
        y = ring(my, d)
        shape = (SIDE, LATENTS, half)
        grads = grad_ref[x].reshape(group, heads * pair)
        da_send[x] = nn(grads, w_t[:, :half]).astype(BF16).reshape(shape)

        @pl.when(d > 0)
        def _():
            for e in order[:3]:
                da_copy(d, e).start()

        grads = grad_ref[:, y].reshape(group, heads * pair)
        db_send[y] = nn(grads, w_t[:, half:]).astype(BF16).reshape(shape)

        @pl.when(d > 0)
        def _():
            for e in order[:3]:
                db_copy(d, e).start()

        return carry

    def latent_send(e):
        for d in peers:
            da_copy(d, e).start()
            db_copy(d, e).start()

    def latent_step(e):
        y = ring(my, e)
        x = ring(mx, e)
        for d in peers:
            da_copy(d, e).wait_recv()
        total = da_send[mx, y].astype(F32)
        for d in peers:
            total = total + da_recv[d - 1, y].astype(F32)
        ea_send[y] = total.astype(BF16)
        if e:
            ea_copy(e).start()
        for d in peers:
            db_copy(d, e).wait_recv()
        total = db_send[my, x].astype(F32)
        for d in peers:
            total = total + db_recv[d - 1, x].astype(F32)
        eb_send[x] = total.astype(BF16)
        if e:
            eb_copy(e).start()

    key_value_grads(0)
    weight_grad(0, other_rows)
    core_copy(0).start()
    weight_grad(0, own_rows)
    core_sum(0)
    z_sum(0)

    key_value_grads(1)
    weight_grad(1, other_rows)
    core_copy(1).start()
    lax.fori_loop(0, SIDE, latent_grads, 0)
    weight_grad(1, own_rows)
    core_sum(1)
    hand_over(0)
    latent_step(1)
    z_sum(1)
    latent_step(3)
    latent_send(0)
    weight_out(0)
    latent_step(2)
    hand_over(1)
    latent_step(0)
    for d in peers:
        ea_copy(d).wait_recv()
    total = ea_send[my].astype(F32)
    for d in peers:
        total = total + ea_recv[d - 1].astype(F32)
    dlat_ref[:, :half] = total.astype(BF16)
    for d in peers:
        eb_copy(d).wait_recv()
    total = eb_send[mx].astype(F32)
    for d in peers:
        total = total + eb_recv[d - 1].astype(F32)
    dlat_ref[:, half:] = total.astype(BF16)
    weight_out(1)

    for d in peers:
        x_first(d).wait_send()
        y_first(d).wait_send()
        ea_copy(d).wait_send()
        eb_copy(d).wait_send()
        for s in (0, *peers):
            da_copy(d, s).wait_send()
            db_copy(d, s).wait_send()
        for head in range(heads):
            z_copy(head, d).wait_send()
            g_copy(head, d).wait_send()
    for head in range(heads):
        core_copy(head).wait_send()
        for d in range(SIDE):
            h_copy(head, d).wait_send()

    for kind in range(2):
        for hop in range(4):
            for s in range(SIDE):
                second(kind, s, hop).wait_send()

    def drain(n, carry):
        @pl.when(lax.rem(n, SEQ) > 0)
        def _():
            forward(n).wait_send()
            backward(n).wait_send()

        return carry

    lax.fori_loop(0, heads * SEQ, drain, 0)


def whole_call(positions, slots, latents, k_weight, v_weight, queries, cotangents):
    tokens, width = queries.shape
    model, cols = k_weight.shape
    heads = cols // HD
    steps = heads * SEQ
    pair = 2 * HD
    half = model // 2
    piece = half // SIDE
    others = SIDE - 1
    smem = pl.BlockSpec(memory_space=pltpu.SMEM)
    vmem = pl.BlockSpec(memory_space=pltpu.VMEM)
    hbm = pl.BlockSpec(memory_space=pl.ANY)
    dma = pltpu.SemaphoreType.DMA
    return pl.pallas_call(
        whole_kernel,
        name="whole",
        out_shape=(
            pltpu.VMEM((tokens, width), BF16),
            pltpu.VMEM((tokens, width), BF16),
            pltpu.VMEM((LATENTS, model), BF16),
            pltpu.VMEM((model, cols), F32),
            pltpu.VMEM((model, cols), F32),
        ),
        in_specs=[smem, smem, hbm, hbm, hbm, hbm, hbm],
        out_specs=(vmem,) * 5,
        scratch_shapes=[
            pltpu.VMEM((SIDE, SIDE, LATENTS, model), BF16),
            pltpu.VMEM((model, SEQ * LATENTS), BF16),
            pltpu.VMEM((model, heads * pair), BF16),
            pltpu.VMEM((heads * pair, model), BF16),
            pltpu.VMEM((heads, SEQ * LATENTS, HD), F32),
            pltpu.VMEM((heads, SEQ * LATENTS, HD), F32),
            pltpu.VMEM((SEQ, LATENTS, heads * pair), BF16),
            pltpu.VMEM((steps, ROWS, pair), BF16),
            pltpu.VMEM((steps, ROWS, pair), BF16),
            pltpu.VMEM((steps, ROWS, pair), BF16),
            pltpu.VMEM((steps, ROWS, pair), BF16),
            pltpu.VMEM((SEQ * NEED, LATENTS, pair), F32),
            pltpu.VMEM((SIDE, SIDE, LATENTS, heads * pair), BF16),
            pltpu.VMEM((1, tokens), jnp.int32),
            pltpu.SMEM((SEQ,), jnp.int32),
            pltpu.SMEM((SEQ,), jnp.int32),
            pltpu.SMEM((SEQ * NEED,), jnp.int32),
            pltpu.VMEM((heads, model, pair), BF16),
            pltpu.VMEM((heads, half, pair), BF16),
            pltpu.VMEM((heads, half, pair), BF16),
            pltpu.VMEM((heads, others, piece, pair), BF16),
            pltpu.VMEM((heads, model, pair), BF16),
            pltpu.VMEM((SIDE, SIDE, LATENTS, half), BF16),
            pltpu.VMEM((SIDE, SIDE, LATENTS, half), BF16),
            pltpu.VMEM((others, SIDE, LATENTS, half), BF16),
            pltpu.VMEM((others, SIDE, LATENTS, half), BF16),
            pltpu.VMEM((SIDE, LATENTS, half), BF16),
            pltpu.VMEM((SIDE, LATENTS, half), BF16),
            pltpu.VMEM((others, LATENTS, half), BF16),
            pltpu.VMEM((others, LATENTS, half), BF16),
            dma((2, SIDE)),
            dma((2, SIDE)),
            dma((2, SIDE, SIDE)),
            dma((2, SIDE, SIDE)),
            dma((steps,)),
            dma((steps,)),
            dma((steps,)),
            dma((steps,)),
            dma((SIDE, 2)),
            dma((1 + 2 * heads,)),
            dma((heads,)),
            dma((heads,)),
            dma((heads, SIDE)),
            dma((heads, SIDE)),
            dma((heads, SIDE)),
            dma((heads, SIDE)),
            dma((heads, SIDE)),
            dma((heads, SIDE)),
            dma((4, SIDE, SIDE)),
            dma((4, SIDE, SIDE)),
        ],
        compiler_params=pltpu.CompilerParams(
            collective_id=0, has_side_effects=True, vmem_limit_bytes=46 * 2**20
        ),
    )(positions, slots, latents, k_weight, v_weight, queries, cotangents)


def finish_kernel(
    ctx_in, dq_in, dk_in, dv_in, dlat_in, ctx_out, dq_out, dk_out, dv_out, dlat_out, sems, lat_sem
):
    copies = [pltpu.make_async_copy(dlat_in, dlat_out, lat_sem)]
    parts = sems.shape[1]
    pairs = ((ctx_in, ctx_out), (dq_in, dq_out), (dk_in, dk_out), (dv_in, dv_out))
    for j, (src, dst) in enumerate(pairs):
        size = src.shape[0] // parts
        for i in range(parts):
            rows = pl.ds(i * size, size)
            copies.append(pltpu.make_async_copy(src.at[rows], dst.at[rows], sems.at[j, i]))
    for copy in copies:
        copy.start()
    for copy in copies:
        copy.wait()


def finish_call(context, d_queries, d_k, d_v, d_latents):
    hbm = pl.BlockSpec(memory_space=pl.ANY)
    dma = pltpu.SemaphoreType.DMA
    whole = jax.ShapeDtypeStruct(context.shape, BF16)
    return pl.pallas_call(
        finish_kernel,
        name="finish",
        out_shape=(
            whole,
            whole,
            jax.ShapeDtypeStruct(d_k.shape, F32),
            jax.ShapeDtypeStruct(d_v.shape, F32),
            jax.ShapeDtypeStruct(d_latents.shape, BF16),
        ),
        in_specs=[hbm] * 5,
        out_specs=(hbm,) * 5,
        scratch_shapes=[
            dma((4, 4)),
            dma(()),
        ],
        compiler_params=pltpu.CompilerParams(vmem_limit_bytes=4 * 2**20),
    )(context, d_queries, d_k, d_v, d_latents)


def local(queries, latents, k_weight, v_weight, d_context, image_pos, image_slot):
    context, d_queries, d_latents, d_k, d_v = whole_call(
        image_pos, image_slot, latents[0, 0], k_weight, v_weight, queries[0], d_context[0]
    )
    context, d_queries, d_k, d_v, d_latents = finish_call(context, d_queries, d_k, d_v, d_latents)
    return context[None], d_queries[None], d_latents[None, None], d_k, d_v


def solution(mesh):
    in_specs = (
        P("dp", "seq", None),
        P("dp", "seq", None, None),
        P(None, "seq"),
        P(None, "seq"),
        P("dp", "seq", None),
        P("dp", None),
        P("dp", None),
    )
    out_specs = (
        P("dp", "seq", None),
        P("dp", "seq", None),
        P("dp", "seq", None, None),
        P(None, "seq"),
        P(None, "seq"),
    )
    return jax.shard_map(local, mesh=mesh, in_specs=in_specs, out_specs=out_specs, check_vma=False)
```

```python
import math

import jax
import jax.numpy as jnp
from jax import lax
from jax.experimental import pallas as pl
from jax.experimental.pallas import tpu as pltpu
from jax.sharding import PartitionSpec as P

HD = 128
LATENTS = 64
NEED = 3
SIDE = 4
SEQ = 16
ROWS = NEED * LATENTS
EPSILON = 1e-06
SCALE = 1.0 / math.sqrt(HD)
MESH = pl.DeviceIdType.MESH
F32 = jnp.float32
BF16 = jnp.bfloat16

OFFSETS = (
    (0, 0),
    (1, 0),
    (3, 0),
    (0, 1),
    (0, 3),
    (2, 0),
    (0, 2),
    (1, 1),
    (3, 3),
    (1, 3),
    (3, 1),
    (2, 1),
    (1, 2),
    (2, 3),
    (3, 2),
    (2, 2),
)
X_CODE = sum(o[0] << (2 * i) for i, o in enumerate(OFFSETS[1:]))
Y_CODE = sum(o[1] << (2 * i) for i, o in enumerate(OFFSETS[1:]))


def offset_of(step):
    place = 2 * lax.rem(step + SEQ - 1, SEQ)
    return (
        lax.rem(lax.shift_right_logical(jnp.int32(X_CODE), place), SIDE),
        lax.rem(lax.shift_right_logical(jnp.int32(Y_CODE), place), SIDE),
    )


def nt(a, b):
    return lax.dot_general(a, b, (((1,), (1,)), ((), ())), preferred_element_type=F32)


def tn(a, b):
    return lax.dot_general(a, b, (((0,), (0,)), ((), ())), preferred_element_type=F32)


def nn(a, b):
    return lax.dot_general(a, b, (((1,), (0,)), ((), ())), preferred_element_type=F32)


def mean_last(a):
    return jnp.mean(a, axis=-1, keepdims=True)


def attend_half(query, cotangent, keys, values, image):
    raw = query.astype(F32)
    inverse = lax.rsqrt(mean_last(raw * raw) + EPSILON)
    unit = raw * inverse
    unit_b = unit.astype(BF16)
    is0, is1, is2 = image == 0, image == 1, image == 2

    def choose(wide):
        return jnp.where(
            is0, wide[:LATENTS], jnp.where(is1, wide[LATENTS : 2 * LATENTS], wide[2 * LATENTS :])
        )

    def widen(narrow):
        return jnp.concatenate(
            [jnp.where(own, narrow, 0.0).astype(BF16) for own in (is0, is1, is2)], axis=0
        )

    exponent = jnp.exp(choose(nt(keys, unit_b)) * SCALE)
    probs = exponent * (1.0 / jnp.sum(exponent, axis=0, keepdims=True))
    dprob = choose(nt(values, cotangent))
    dscore = probs * (dprob - jnp.sum(probs * dprob, axis=0, keepdims=True)) * SCALE
    probs_wide = widen(probs)
    dscore_wide = widen(dscore)
    context = tn(probs_wide, values)
    query_cot = tn(dscore_wide, keys)
    d_query = inverse * (query_cot - unit * mean_last(query_cot * unit))
    return (
        context.astype(BF16),
        d_query.astype(BF16),
        nn(dscore_wide, unit_b),
        nn(probs_wide, cotangent),
    )


def whole_kernel(
    pos_ref, slot_ref, lat_hbm, kw_hbm, vw_hbm, q_hbm, c_hbm,
    c_buf, q_buf, dlat_ref, dk_ref, dv_ref,
    lat_all, lat_t, w_ref, w_t, unit_ref, inv_ref, kv_ref, kv_send, kv_recv, g_send, g_recv, run_ref, grad_ref, img_ref,
    first_ref, last_ref, keep_ref,
    dw_send, core_recv, z_send, z_recv, final_ref,
    da_send, db_send, da_recv, db_recv, ea_send, eb_send, ea_recv, eb_recv,
    l_ss, l_rs, m_ss, m_rs, f_ss, f_rs, b_ss, b_rs, q_sem, in_sem,
    core_ss, core_rs, z_ss, z_rs, g_ss, g_rs, h_ss, h_rs, d_ss, d_rs,
):
    tokens = q_hbm.shape[0]
    model = lat_hbm.shape[1]
    cols = kw_hbm.shape[1]
    heads = cols // HD
    pair = 2 * HD
    half = model // 2
    piece = half // SIDE
    group = SIDE * LATENTS
    peers = (1, 3, 2)
    dp = lax.axis_index("dp")
    me = lax.axis_index("seq")
    mx = lax.div(me, SIDE)
    my = lax.rem(me, SIDE)
    mz = lax.div(dp, 2)
    core = lax.rem(dp, 2)

    def ring(base, d):
        return lax.rem(base + d, SIDE)

    def peer(dx, dy):
        return (dp, ring(mx, dx) * SIDE + ring(my, dy))

    def z_peer(d):
        return (ring(mz, d) * 2 + core, me)

    core_peer = (mz * 2 + 1 - core, me)

    def owner_of(step):
        dx, dy = offset_of(step)
        return ring(mx, SIDE - dx) * SIDE + ring(my, SIDE - dy)

    def remote(src, dst, send_sem, recv_sem, device):
        return pltpu.make_async_remote_copy(
            src_ref=src,
            dst_ref=dst,
            send_sem=send_sem,
            recv_sem=recv_sem,
            device_id=device,
            device_id_type=MESH,
        )

    def lanes_of(n):
        place = owner_of(lax.rem(n, SEQ)) * cols + lax.div(n, SEQ) * HD
        return pl.ds(pl.multiple_of(place, HD), HD)

    def fetch(i, j):
        rows = pl.ds(i * (tokens // SIDE), tokens // SIDE)
        src, dst = ((q_hbm, q_buf), (c_hbm, c_buf))[j]
        return pltpu.make_async_copy(src.at[rows], dst.at[rows], q_sem.at[i, j])

    barrier = pltpu.get_barrier_semaphore()
    for dx, dy in OFFSETS[1:]:
        pl.semaphore_signal(barrier, inc=1, device_id=peer(dx, dy), device_id_type=MESH)
    for d in peers:
        pl.semaphore_signal(barrier, inc=1, device_id=z_peer(d), device_id_type=MESH)
    pl.semaphore_signal(barrier, inc=1, device_id=core_peer, device_id_type=MESH)

    low = pl.ds(0, LATENTS // 2)
    high = pl.ds(LATENTS // 2, LATENTS // 2)

    def x_first(d):
        return remote(
            lat_hbm.at[low], lat_all.at[mx, my, low], l_ss.at[0, d], l_rs.at[0, d], peer(d, 0)
        )

    def y_first(d):
        return remote(
            lat_hbm.at[high], lat_all.at[mx, my, high], l_ss.at[1, d], l_rs.at[1, d], peer(0, d)
        )

    part_rows = LATENTS // 4
    hops = ((0, 1, 0, 2), (0, 3, 0, 2), (1, 1, 0, 1), (3, 3, 1, 1))

    def second(kind, s, hop):
        back, d, begin, parts = hops[hop]
        rows = pl.ds((2 * kind + begin) * part_rows, parts * part_rows)
        x, y = ((s, back), (back, s))[kind]
        block = lat_all.at[ring(mx, SIDE - x), ring(my, SIDE - y), rows]
        source = lat_hbm.at[rows] if back == 0 and s == 0 else block
        target = peer(d, 0) if kind else peer(0, d)
        return remote(source, block, m_ss.at[kind, s, hop], m_rs.at[kind, s, hop], target)

    def spread(s):
        for hop in (0, 1):
            for kind in range(2):
                second(kind, s, hop).start()

    def pass_on(s):
        for hop in (0, 1):
            for kind in range(2):
                second(kind, s, hop).wait_recv()
                second(kind, s, hop + 2).start()

    copies = [pltpu.make_async_copy(lat_hbm, lat_all.at[mx, my], in_sem.at[0])]
    for head in range(heads):
        for i, src in enumerate((kw_hbm, vw_hbm)):
            copies.append(
                pltpu.make_async_copy(
                    src.at[:, pl.ds(head * HD, HD)],
                    w_ref.at[:, pl.ds(head * pair + i * HD, HD)],
                    in_sem.at[1 + 2 * head + i],
                )
            )
    for copy in copies:
        copy.start()
    pl.semaphore_wait(barrier, SEQ - 1 + SIDE)
    for d in peers:
        x_first(d).start()
        y_first(d).start()
    spread(0)

    for i in range(SIDE):
        for j in range(2):
            fetch(i, j).start()

    def block_images(block, carry):
        count = jnp.int32(-1)
        for i in range(SEQ):
            count = count + (pos_ref[0, i] <= block * tokens).astype(jnp.int32)
        first_ref[block] = count
        return carry

    lax.fori_loop(0, SEQ, block_images, 0)

    def slot_last(slot, carry):
        image = jnp.int32(0)
        for i in range(SEQ):
            image = image + jnp.where(slot_ref[0, i] == slot, i, 0)
        image = jnp.minimum(image, SEQ - 1)
        after = pos_ref[0, jnp.minimum(image + 1, SEQ - 1)]
        end = jnp.where(image == SEQ - 1, SEQ * tokens, after) - 1
        block = jnp.maximum(lax.div(end, tokens), 0)
        place = jnp.clip(image - first_ref[block], 0, NEED - 1)
        last_ref[slot] = block * NEED + place
        return carry

    lax.fori_loop(0, SEQ, slot_last, 0)

    token = me * tokens + lax.broadcasted_iota(jnp.int32, (1, tokens), 1)
    seen = jnp.zeros((1, tokens), jnp.int32) - 1 - first_ref[me]
    for i in range(SEQ):
        seen = seen + (token >= pos_ref[0, i]).astype(jnp.int32)
    img_ref[...] = seen

    for s, settled in ((1, 0), (3, 1), (2, 3)):
        x_first(s).wait_recv()
        y_first(s).wait_recv()
        spread(s)
        pass_on(settled)
    pass_on(2)
    for s in range(SIDE):
        for kind in range(2):
            second(kind, s, 2).wait_recv()
            second(kind, s, 3).wait_recv()
    for copy in copies:
        copy.wait()

    def project(x, carry):
        rows = pl.ds(pl.multiple_of(x * group, group), group)
        slots = pl.ds(x * SIDE, SIDE)
        raw = nn(lat_all[x].reshape(group, model), w_ref[...])
        for head in range(heads):
            one = raw[:, head * pair : head * pair + HD]
            inverse = lax.rsqrt(mean_last(one * one) + EPSILON)
            unit = one * inverse
            unit_ref[head, rows, :] = unit
            inv_ref[head, rows, :] = jnp.broadcast_to(inverse, unit.shape)
            kv_ref[slots, :, head * pair : head * pair + HD] = unit.astype(BF16).reshape(
                SIDE, LATENTS, HD
            )
            values = raw[:, head * pair + HD : (head + 1) * pair].astype(BF16)
            kv_ref[slots, :, head * pair + HD : (head + 1) * pair] = values.reshape(
                SIDE, LATENTS, HD
            )
        return carry

    lax.fori_loop(0, SIDE, project, 0)

    def forward(n):
        dx, dy = offset_of(lax.rem(n, SEQ))
        return remote(kv_send.at[n], kv_recv.at[n], f_ss.at[n], f_rs.at[n], peer(dx, dy))

    def backward(n):
        place = lax.div(n, SEQ) * SEQ + me
        return remote(
            g_send.at[n],
            g_recv.at[place],
            b_ss.at[n],
            b_rs.at[place],
            (dp, owner_of(lax.rem(n, SEQ))),
        )

    def arrival(n):
        return remote(g_send.at[0], g_recv.at[n], b_ss.at[0], b_rs.at[n], (dp, lax.rem(n, SEQ)))

    def prepare(target, n, head, block):
        for j in range(NEED):
            slot = slot_ref[0, jnp.minimum(first_ref[block] + j, SEQ - 1)]
            both = kv_ref[slot]
            target[n, j * LATENTS : (j + 1) * LATENTS, :] = both[:, head * pair : (head + 1) * pair]

    for head in range(heads):

        def send(step, carry, head=head):
            n = head * SEQ + step
            dx, dy = offset_of(step)
            prepare(kv_send, n, head, peer(dx, dy)[1])
            forward(n).start()
            return carry

        lax.fori_loop(1, SEQ, send, 0)
    for head in range(heads):
        prepare(kv_recv, head * SEQ, head, me)

    def turn(x, carry):
        rows = pl.ds(pl.multiple_of(x * group, group), group)
        lat_t[:, rows] = lat_all[x].reshape(group, model).T
        return carry

    lax.fori_loop(0, SIDE, turn, 0)
    w_t[...] = w_ref[...].T

    def keep_flags(block, carry):
        first = first_ref[block]
        end = (block + 1) * tokens - 1
        before = block * tokens - 1
        last = jnp.int32(-1)
        previous = jnp.int32(-1)
        for i in range(SEQ):
            last = last + (pos_ref[0, i] <= end).astype(jnp.int32)
            previous = previous + (pos_ref[0, i] <= before).astype(jnp.int32)
        for j in range(NEED):
            same = previous == first if j == 0 else first + j > last
            keep_ref[block * NEED + j] = same.astype(jnp.int32)
        return carry

    lax.fori_loop(0, SEQ, keep_flags, 0)

    for i in range(SIDE):
        for j in range(2):
            fetch(i, j).wait()

    def attend(n, carry):
        own = lax.rem(n, SEQ) == 0

        @pl.when(jnp.logical_not(own))
        def _():
            forward(n).wait_recv()

        lanes = lanes_of(n)
        keys = kv_recv[n, :, :HD]
        values = kv_recv[n, :, HD:]
        key_part = jnp.zeros((ROWS, HD), F32)
        value_part = jnp.zeros((ROWS, HD), F32)
        size = 256
        for begin in range(0, tokens, size):
            rows = slice(begin, begin + size)
            context, d_query, key_add, value_add = attend_half(
                q_buf[rows, lanes], c_buf[rows, lanes], keys, values, img_ref[:, rows]
            )
            c_buf[rows, lanes] = context
            q_buf[rows, lanes] = d_query
            key_part = key_part + key_add
            value_part = value_part + value_add
        g_send[n, :, :HD] = key_part.astype(BF16)
        g_send[n, :, HD:] = value_part.astype(BF16)

        @pl.when(jnp.logical_not(own))
        def _():
            backward(n).start()

        @pl.when(own)
        def _():
            g_recv[lax.div(n, SEQ) * SEQ + me] = g_send[n]

        return carry

    lax.fori_loop(0, heads * SEQ, attend, 0)

    def key_value_grads(head):
        def combine(block, run):
            @pl.when(block != me)
            def _():
                arrival(head * SEQ + block).wait_recv()

            for j in range(NEED):
                keep = keep_ref[block * NEED + j].astype(F32)
                part = g_recv[head * SEQ + block, j * LATENTS : (j + 1) * LATENTS, :]
                run = run * keep + part.astype(F32)
                run_ref[block * NEED + j] = run
            return run

        lax.fori_loop(0, SEQ, combine, jnp.zeros((LATENTS, pair), F32))

        def finish(x, carry):
            rows = pl.ds(pl.multiple_of(x * group, group), group)
            total = jnp.concatenate([run_ref[last_ref[x * SIDE + y]] for y in range(SIDE)], axis=0)
            cot = total[:, :HD]
            unit = unit_ref[head, rows, :]
            key_grad = inv_ref[head, rows, :] * (cot - unit * mean_last(cot * unit))
            shape = (SIDE, LATENTS, HD)
            lanes = slice(head * pair, head * pair + HD)
            grad_ref[x, :, :, lanes] = key_grad.astype(BF16).reshape(shape)
            lanes = slice(head * pair + HD, (head + 1) * pair)
            grad_ref[x, :, :, lanes] = total[:, HD:].astype(BF16).reshape(shape)
            return carry

        lax.fori_loop(0, SIDE, finish, 0)

    own_rows = pl.multiple_of(core * half, half)
    other_rows = pl.multiple_of((1 - core) * half, half)

    def weight_grad(head, base):
        chunk = half // 2

        def one(i, carry):
            rows = pl.ds(pl.multiple_of(base + i * chunk, chunk), chunk)
            grads = grad_ref[:, :, :, head * pair : (head + 1) * pair]
            grads = grads.reshape(SEQ * LATENTS, pair)
            dw_send[head, rows, :] = nn(lat_t[rows, :], grads).astype(BF16)
            return carry

        lax.fori_loop(0, half // chunk, one, 0)

    def core_copy(head):
        return remote(
            dw_send.at[head, pl.ds(other_rows, half)],
            core_recv.at[head],
            core_ss.at[head],
            core_rs.at[head],
            core_peer,
        )

    def z_copy(head, d):
        rows = pl.ds(pl.multiple_of(ring(mz, d) * piece, piece), piece)
        return remote(
            z_send.at[head, rows],
            z_recv.at[head, d - 1],
            z_ss.at[head, d],
            z_rs.at[head, d],
            z_peer(d),
        )

    def final_rows(z, c):
        return pl.ds(pl.multiple_of(c * half + z * piece, piece), piece)

    def g_copy(head, d):
        block = final_ref.at[head, final_rows(mz, core)]
        return remote(block, block, g_ss.at[head, d], g_rs.at[head, d], z_peer(d))

    def h_copy(head, d):
        block = final_ref.at[head, final_rows(ring(mz, SIDE - d), core)]
        return remote(block, block, h_ss.at[head, d], h_rs.at[head, d], core_peer)

    def core_sum(head):
        core_copy(head).wait_recv()

        def one(i, carry):
            rows = pl.ds(pl.multiple_of(i * piece, piece), piece)
            own = pl.ds(pl.multiple_of(own_rows + i * piece, piece), piece)
            total = dw_send[head, own, :].astype(F32) + core_recv[head, rows, :].astype(F32)
            z_send[head, rows, :] = total.astype(BF16)
            return carry

        lax.fori_loop(0, SIDE, one, 0)
        for d in peers:
            z_copy(head, d).start()

    def z_sum(head):
        for d in peers:
            z_copy(head, d).wait_recv()
        total = z_send[head, pl.ds(pl.multiple_of(mz * piece, piece), piece), :].astype(F32)
        for d in peers:
            total = total + z_recv[head, d - 1].astype(F32)
        final_ref[head, final_rows(mz, core), :] = total.astype(BF16)
        for d in peers:
            g_copy(head, d).start()
        h_copy(head, 0).start()

    def hand_over(head):
        for d in peers:
            g_copy(head, d).wait_recv()
            h_copy(head, d).start()

    def weight_out(head):
        for d in range(SIDE):
            h_copy(head, d).wait_recv()
        lanes = slice(head * HD, (head + 1) * HD)

        def one(i, carry):
            rows = pl.ds(pl.multiple_of(i * piece, piece), piece)
            both = final_ref[head, rows, :].astype(F32)
            dk_ref[rows, lanes] = both[:, :HD]
            dv_ref[rows, lanes] = both[:, HD:]
            return carry

        lax.fori_loop(0, 2 * SIDE, one, 0)

    def da_copy(d, e):
        y = ring(my, e)
        return remote(
            da_send.at[ring(mx, d), y],
            da_recv.at[d - 1, y],
            d_ss.at[0, d, e],
            d_rs.at[0, d, e],
            peer(d, 0),
        )

    def db_copy(d, e):
        x = ring(mx, e)
        return remote(
            db_send.at[ring(my, d), x],
            db_recv.at[d - 1, x],
            d_ss.at[1, d, e],
            d_rs.at[1, d, e],
            peer(0, d),
        )

    def ea_copy(d):
        return remote(
            ea_send.at[ring(my, d)], ea_recv.at[d - 1], d_ss.at[2, 0, d], d_rs.at[2, 0, d], peer(0, d)
        )

    def eb_copy(d):
        return remote(
            eb_send.at[ring(mx, d)], eb_recv.at[d - 1], d_ss.at[3, 0, d], d_rs.at[3, 0, d], peer(d, 0)
        )

    order = (*peers, 0)

    def latent_grads(i, carry):
        d = lax.rem(i + 1, SIDE)
        x = ring(mx, d)
        y = ring(my, d)
        shape = (SIDE, LATENTS, half)
        grads = grad_ref[x].reshape(group, heads * pair)
        da_send[x] = nn(grads, w_t[:, :half]).astype(BF16).reshape(shape)

        @pl.when(d > 0)
        def _():
            for e in order[:3]:
                da_copy(d, e).start()

        grads = grad_ref[:, y].reshape(group, heads * pair)
        db_send[y] = nn(grads, w_t[:, half:]).astype(BF16).reshape(shape)

        @pl.when(d > 0)
        def _():
            for e in order[:3]:
                db_copy(d, e).start()

        return carry

    def latent_send(e):
        for d in peers:
            da_copy(d, e).start()
            db_copy(d, e).start()

    def latent_step(e):
        y = ring(my, e)
        x = ring(mx, e)
        for d in peers:
            da_copy(d, e).wait_recv()
        total = da_send[mx, y].astype(F32)
        for d in peers:
            total = total + da_recv[d - 1, y].astype(F32)
        ea_send[y] = total.astype(BF16)
        if e:
            ea_copy(e).start()
        for d in peers:
            db_copy(d, e).wait_recv()
        total = db_send[my, x].astype(F32)
        for d in peers:
            total = total + db_recv[d - 1, x].astype(F32)
        eb_send[x] = total.astype(BF16)
        if e:
            eb_copy(e).start()

    key_value_grads(0)
    weight_grad(0, other_rows)
    core_copy(0).start()
    weight_grad(0, own_rows)
    core_sum(0)

    key_value_grads(1)
    weight_grad(1, other_rows)
    core_copy(1).start()
    z_sum(0)
    lax.fori_loop(0, SIDE, latent_grads, 0)
    weight_grad(1, own_rows)
    core_sum(1)
    latent_step(1)
    hand_over(0)
    z_sum(1)
    latent_step(3)
    latent_send(0)
    weight_out(0)
    latent_step(2)
    hand_over(1)
    latent_step(0)
    for d in peers:
        ea_copy(d).wait_recv()
    total = ea_send[my].astype(F32)
    for d in peers:
        total = total + ea_recv[d - 1].astype(F32)
    dlat_ref[:, :half] = total.astype(BF16)
    for d in peers:
        eb_copy(d).wait_recv()
    total = eb_send[mx].astype(F32)
    for d in peers:
        total = total + eb_recv[d - 1].astype(F32)
    dlat_ref[:, half:] = total.astype(BF16)
    weight_out(1)

    for d in peers:
        x_first(d).wait_send()
        y_first(d).wait_send()
        ea_copy(d).wait_send()
        eb_copy(d).wait_send()
        for s in (0, *peers):
            da_copy(d, s).wait_send()
            db_copy(d, s).wait_send()
        for head in range(heads):
            z_copy(head, d).wait_send()
            g_copy(head, d).wait_send()
    for head in range(heads):
        core_copy(head).wait_send()
        for d in range(SIDE):
            h_copy(head, d).wait_send()

    for kind in range(2):
        for hop in range(4):
            for s in range(SIDE):
                second(kind, s, hop).wait_send()

    def drain(n, carry):
        @pl.when(lax.rem(n, SEQ) > 0)
        def _():
            forward(n).wait_send()
            backward(n).wait_send()

        return carry

    lax.fori_loop(0, heads * SEQ, drain, 0)


def whole_call(positions, slots, latents, k_weight, v_weight, queries, cotangents):
    tokens, width = queries.shape
    model, cols = k_weight.shape
    heads = cols // HD
    steps = heads * SEQ
    pair = 2 * HD
    half = model // 2
    piece = half // SIDE
    others = SIDE - 1
    smem = pl.BlockSpec(memory_space=pltpu.SMEM)
    vmem = pl.BlockSpec(memory_space=pltpu.VMEM)
    hbm = pl.BlockSpec(memory_space=pl.ANY)
    dma = pltpu.SemaphoreType.DMA
    return pl.pallas_call(
        whole_kernel,
        name="whole",
        out_shape=(
            pltpu.VMEM((tokens, width), BF16),
            pltpu.VMEM((tokens, width), BF16),
            pltpu.VMEM((LATENTS, model), BF16),
            pltpu.VMEM((model, cols), F32),
            pltpu.VMEM((model, cols), F32),
        ),
        in_specs=[smem, smem, hbm, hbm, hbm, hbm, hbm],
        out_specs=(vmem,) * 5,
        scratch_shapes=[
            pltpu.VMEM((SIDE, SIDE, LATENTS, model), BF16),
            pltpu.VMEM((model, SEQ * LATENTS), BF16),
            pltpu.VMEM((model, heads * pair), BF16),
            pltpu.VMEM((heads * pair, model), BF16),
            pltpu.VMEM((heads, SEQ * LATENTS, HD), F32),
            pltpu.VMEM((heads, SEQ * LATENTS, HD), F32),
            pltpu.VMEM((SEQ, LATENTS, heads * pair), BF16),
            pltpu.VMEM((steps, ROWS, pair), BF16),
            pltpu.VMEM((steps, ROWS, pair), BF16),
            pltpu.VMEM((steps, ROWS, pair), BF16),
            pltpu.VMEM((steps, ROWS, pair), BF16),
            pltpu.VMEM((SEQ * NEED, LATENTS, pair), F32),
            pltpu.VMEM((SIDE, SIDE, LATENTS, heads * pair), BF16),
            pltpu.VMEM((1, tokens), jnp.int32),
            pltpu.SMEM((SEQ,), jnp.int32),
            pltpu.SMEM((SEQ,), jnp.int32),
            pltpu.SMEM((SEQ * NEED,), jnp.int32),
            pltpu.VMEM((heads, model, pair), BF16),
            pltpu.VMEM((heads, half, pair), BF16),
            pltpu.VMEM((heads, half, pair), BF16),
            pltpu.VMEM((heads, others, piece, pair), BF16),
            pltpu.VMEM((heads, model, pair), BF16),
            pltpu.VMEM((SIDE, SIDE, LATENTS, half), BF16),
            pltpu.VMEM((SIDE, SIDE, LATENTS, half), BF16),
            pltpu.VMEM((others, SIDE, LATENTS, half), BF16),
            pltpu.VMEM((others, SIDE, LATENTS, half), BF16),
            pltpu.VMEM((SIDE, LATENTS, half), BF16),
            pltpu.VMEM((SIDE, LATENTS, half), BF16),
            pltpu.VMEM((others, LATENTS, half), BF16),
            pltpu.VMEM((others, LATENTS, half), BF16),
            dma((2, SIDE)),
            dma((2, SIDE)),
            dma((2, SIDE, SIDE)),
            dma((2, SIDE, SIDE)),
            dma((steps,)),
            dma((steps,)),
            dma((steps,)),
            dma((steps,)),
            dma((SIDE, 2)),
            dma((1 + 2 * heads,)),
            dma((heads,)),
            dma((heads,)),
            dma((heads, SIDE)),
            dma((heads, SIDE)),
            dma((heads, SIDE)),
            dma((heads, SIDE)),
            dma((heads, SIDE)),
            dma((heads, SIDE)),
            dma((4, SIDE, SIDE)),
            dma((4, SIDE, SIDE)),
        ],
        compiler_params=pltpu.CompilerParams(
            collective_id=0, has_side_effects=True, vmem_limit_bytes=46 * 2**20
        ),
    )(positions, slots, latents, k_weight, v_weight, queries, cotangents)


def finish_kernel(
    ctx_in, dq_in, dk_in, dv_in, dlat_in, ctx_out, dq_out, dk_out, dv_out, dlat_out, sems, lat_sem
):
    copies = [pltpu.make_async_copy(dlat_in, dlat_out, lat_sem)]
    parts = sems.shape[1]
    pairs = ((ctx_in, ctx_out), (dq_in, dq_out), (dk_in, dk_out), (dv_in, dv_out))
    for j, (src, dst) in enumerate(pairs):
        size = src.shape[0] // parts
        for i in range(parts):
            rows = pl.ds(i * size, size)
            copies.append(pltpu.make_async_copy(src.at[rows], dst.at[rows], sems.at[j, i]))
    for copy in copies:
        copy.start()
    for copy in copies:
        copy.wait()


def finish_call(context, d_queries, d_k, d_v, d_latents):
    hbm = pl.BlockSpec(memory_space=pl.ANY)
    dma = pltpu.SemaphoreType.DMA
    whole = jax.ShapeDtypeStruct(context.shape, BF16)
    return pl.pallas_call(
        finish_kernel,
        name="finish",
        out_shape=(
            whole,
            whole,
            jax.ShapeDtypeStruct(d_k.shape, F32),
            jax.ShapeDtypeStruct(d_v.shape, F32),
            jax.ShapeDtypeStruct(d_latents.shape, BF16),
        ),
        in_specs=[hbm] * 5,
        out_specs=(hbm,) * 5,
        scratch_shapes=[
            dma((4, 4)),
            dma(()),
        ],
        compiler_params=pltpu.CompilerParams(vmem_limit_bytes=4 * 2**20),
    )(context, d_queries, d_k, d_v, d_latents)


def local(queries, latents, k_weight, v_weight, d_context, image_pos, image_slot):
    context, d_queries, d_latents, d_k, d_v = whole_call(
        image_pos, image_slot, latents[0, 0], k_weight, v_weight, queries[0], d_context[0]
    )
    context, d_queries, d_k, d_v, d_latents = finish_call(context, d_queries, d_k, d_v, d_latents)
    return context[None], d_queries[None], d_latents[None, None], d_k, d_v


def solution(mesh):
    in_specs = (
        P("dp", "seq", None),
        P("dp", "seq", None, None),
        P(None, "seq"),
        P(None, "seq"),
        P("dp", "seq", None),
        P("dp", None),
        P("dp", None),
    )
    out_specs = (
        P("dp", "seq", None),
        P("dp", "seq", None),
        P("dp", "seq", None, None),
        P(None, "seq"),
        P(None, "seq"),
    )
    return jax.shard_map(local, mesh=mesh, in_specs=in_specs, out_specs=out_specs, check_vma=False)
```
